32 devices in a mesh: ens: 2 (over y), lon: 4 (over z), lat: 4 (over x, core).
Axes of the slice: x: 2, y: 2, z: 4, core: 2. Of those that a mesh axis runs over, the one named last changes fastest.
Arguments:
- field: float32 [8, 1440, 640], P(('ens', 'lat'), 'lon'), parts along dimension 0, may hold values from -6 to 6
- piece_lengths: int32 [4], replicated, may hold values from 1 to 360, 720 in all
- offsets: int32 [4], replicated, may hold values from 0 to 2, as said below
- basis: float32 [9, 4, 2, 17], replicated, may hold values from -1 to 1
- depth_weight: float32 [9, 640], replicated, may hold values from -2 to 2
- gain: float32 [640], replicated, may hold values from 0.5 to 1.5
- w_in: bfloat16 [640, 1280], replicated, may hold values from -0.25 to 0.25
- b_in: float32 [1280], replicated, may hold values from -3 to 3
- w_out: bfloat16 [1280, 640], replicated, may hold values from -0.15625 to 0.15625
- b_out: float32 [640], replicated, may hold values from -3 to 3
Outputs:
- result: float32 [8, 1440, 640], P(('ens', 'lat'), 'lon'), parts along dimension 0
The draws below stay inside these ranges and needn't reach their ends.
There are 2 independent parts, one for each index of `ens`. The reference program is written for one: setup_inputs(seed, part) draws one part's arguments, and reference() takes and returns one part's arrays. A program takes and returns all parts, laid end to end along the dimension named above; an argument that names none is the same for every part. Nothing has to cross between parts.
Inputs may be any that keep to these rules, and one draw needn't show every extreme that they name: Index b of lon holds longitudes starts[b] to starts[b] + piece_lengths[b] - 1 in its first piece_lengths[b] slots; the lengths sum to 720. Output row i reads latitude rows offsets[i] to offsets[i] + 1, and i - 1 <= offsets[i] <= i.
All inputs are finite; a program needn't handle non-finite values.
Results may differ from the reference program's by a relative error of at most 0.0018.
Values sent between devices are 32-bit elements; how exact they have to be, the bound alone decides.
A program may use at most 64 MiB of HBM per device.

```python
import math
import jax
import jax.numpy as jnp
import numpy as np
from jax import lax

C = 640
HID = 1280
NLON = 720
NB = 9
LW = 17
NLAT = 4
SPAN = 2
LCAP = 360
N_LON = 4


def draw_offsets(key, part):
    rows = jnp.arange(NLAT, dtype=jnp.int32)
    lag = jax.random.randint(jax.random.fold_in(key, 71), (NLAT,), 0, SPAN, dtype=jnp.int32)
    return jnp.clip(rows - lag, 0, NLAT - SPAN).astype(jnp.int32)


def block_scale(stream_key, shape, split, least, top_value):
    loudness, own = 1.0, jax.random.fold_in(stream_key, 6)
    for position, blocks in split:
        heights = jnp.exp(jax.random.uniform(jax.random.fold_in(own, position), (blocks,), jnp.float32, least / len(split), top_value / len(split)))
        loudness = loudness * jnp.repeat(heights, shape[position] // blocks).reshape([-1 if axis == position else 1 for axis in range(len(shape))])
    return loudness


def length_profile(amount, total, limit, slope):
    portions = [(1 << 20) // math.isqrt(grade ** slope) + 1 for grade in range(2, amount + 1)]
    rest, holding = total - limit - (amount - 1), [1] * (amount - 1)
    while rest > 0:
        free = [i for i in range(amount - 1) if holding[i] < limit]
        pool, remaining = sum([portions[i] for i in free]), rest
        for i in free:
            addition = min(limit - holding[i], max(1, remaining * portions[i] // pool), rest)
            holding[i] = holding[i] + addition
            rest = rest - addition
    return np.array([limit] + holding)


def uneven(key, number_of, total, bound, lean):
    if number_of == 2:
        one = jax.random.randint(key, (), max(1, total - bound), min(bound, total - 1) + 1)
        return jnp.stack([one, total - one])
    lengths = jnp.asarray(length_profile(number_of, total, bound, lean), jnp.int32)
    pairs = (number_of - 1) // 2
    donor, sink = lengths[1:1 + 2 * pairs:2], lengths[2:2 + 2 * pairs:2]
    slack = jnp.minimum(donor - 1, bound - sink)
    passed = jax.random.randint(jax.random.fold_in(key, 1), (pairs,), 0, 1 << 20) % (slack + 1)
    lengths = lengths.at[1:1 + 2 * pairs:2].set(donor - passed).at[2:2 + 2 * pairs:2].set(sink + passed)
    return lengths[jax.random.permutation(jax.random.fold_in(key, 2), number_of)]


def normal_values(rng, dims, deviation, bound, split=(), kind=jnp.bfloat16):
    loudness = block_scale(rng, dims, split, -0.22, 0.18) if split else 1.0
    array = jax.random.normal(rng, dims, jnp.float32) * deviation * loudness
    return jnp.minimum(jnp.maximum(array, -bound), bound).astype(kind)


def setup_inputs(seed: int = 0, part: int = 0) -> dict:
    seeds = jax.random.split(jax.random.key(seed), 11)
    part_splits = jax.random.split(jax.random.fold_in(seeds[10], part), 11)
    field = normal_values(part_splits[0], (NLAT, N_LON * LCAP, C), 1.0, 6.0, ((0, 4), (1, 4)), jnp.float32)
    piece_lengths = uneven(seeds[1], N_LON, NLON, LCAP, 2).astype(jnp.int32)
    offsets = draw_offsets(jax.random.fold_in(seeds[10], 71), part)
    basis = normal_values(seeds[3], (NB, NLAT, SPAN, LW), (SPAN * LW) ** -0.5, 1.0, (), jnp.float32)
    depth_weight = normal_values(seeds[4], (NB, C), 0.3333, 2.0, (), jnp.float32)
    gain = jnp.clip(jax.random.uniform(seeds[5], (C,), jnp.float32, 0.5, 1.5), 0.5, 1.5)
    w_in = normal_values(seeds[6], (C, HID), C ** -0.5, 0.25)
    b_in = normal_values(seeds[7], (HID,), 0.5, 3.0, (), jnp.float32)
    w_out = normal_values(seeds[8], (HID, C), HID ** -0.5, 0.15625)
    b_out = normal_values(seeds[9], (C,), 0.5, 3.0, (), jnp.float32)
    return dict(field=field, piece_lengths=piece_lengths, offsets=offsets, basis=basis, depth_weight=depth_weight, gain=gain, w_in=w_in, b_in=b_in, w_out=w_out, b_out=b_out)


def slot_table(piece_lengths):
    starts = (jnp.cumsum(piece_lengths) - piece_lengths).astype(jnp.int32)
    longitudes = jnp.arange(NLON, dtype=jnp.int32)
    owner = (lax.optimization_barrier(jnp.sum((starts[None, :] <= longitudes[:, None]).astype(jnp.int32), axis=1)) - 1).astype(jnp.int32)
    own_start = lax.optimization_barrier(jnp.sum(jnp.where(jnp.arange(N_LON, dtype=jnp.int32)[None, :] == owner[:, None], starts[None, :], 0), axis=1)).astype(jnp.int32)
    return (owner * LCAP + longitudes - own_start).astype(jnp.int32)

def reference(field, piece_lengths, offsets, basis, depth_weight, gain, w_in, b_in, w_out, b_out):
    slot_index = slot_table(piece_lengths)
    dense = jnp.take(field, slot_index, axis=1)
    coefficients = jnp.einsum('kism,kc->ismc', basis, depth_weight, precision=lax.Precision.HIGHEST)
    half_taps = LW // 2

    def one_row(row):
        support = lax.dynamic_slice_in_dim(dense, offsets[row].astype(jnp.int32), SPAN, 0)
        row_coef = coefficients[row]
        total = jnp.zeros((NLON, C), jnp.float32)
        for tap in range(LW):
            shifted = jnp.roll(support, half_taps - tap, axis=1)
            total = total + lax.optimization_barrier(jnp.sum(row_coef[:, tap, :][:, None, :] * shifted, axis=0))
        return total
    conv = lax.map(one_row, jnp.arange(NLAT, dtype=jnp.int32))
    state = dense + conv
    mean_sq = lax.optimization_barrier(jnp.mean(state * state, axis=-1, keepdims=True))
    normed = (state * lax.rsqrt(mean_sq + 1e-05) * gain).astype(jnp.bfloat16).reshape(-1, C)
    pre = jnp.dot(normed, w_in, preferred_element_type=jnp.float32) + b_in
    activated = jax.nn.gelu(pre, approximate=False).astype(jnp.bfloat16)
    mlp_out = jnp.dot(activated, w_out, preferred_element_type=jnp.float32) + b_out
    output = state + mlp_out.reshape(NLAT, NLON, C)
    result = jnp.zeros(field.shape, jnp.float32).at[:, slot_index, :].set(output)
    return result
```

```python
import functools
import jax
import jax.numpy as jnp
from jax import lax
from jax.experimental import pallas as pl
from jax.experimental.pallas import tpu as pltpu
from jax.sharding import PartitionSpec as P

LANES = 128
HALO = 8
MESH = pl.DeviceIdType.MESH
SQRT_HALF = 0.7071067811865476


def round_up(value, step):
    return -(-value // step) * step


def block_rows(total, most):
    return max(rows for rows in range(8, most + 1, 8) if total % rows == 0)


def kernel(
    groups, lat_count, n, hid_block,
    lengths, offsets, field, basis, depth_weight, gain, w_in_hbm, b_in, w_out_hbm, b_out,
    out_hbm,
    raw, edge, peers, halo, nb, nb_halo, ext, ext_nb, tail, tail_nb, terms, coef, acc, st, out_buf, w_in, w_out,
    load_sem, weight_sem, edge_send, edge_recv, halo_send, halo_recv, row_send, row_recv, out_sem,
):
    cap = raw.shape[1]
    tiles = raw.shape[0]
    channels = tiles * LANES
    taps = basis.shape[3]
    count_k = basis.shape[0]
    blocks = cap // n
    hidden = w_in.shape[1]
    g = lax.axis_index("lon")
    t = lax.axis_index("lat")
    above, below = t < lat_count - 1, t > 0

    loads = [
        pltpu.make_async_copy(field.at[0, :, pl.ds(k * LANES, LANES)], raw.at[k], load_sem.at[k])
        for k in range(tiles)
    ]
    weights = [
        pltpu.make_async_copy(w_in_hbm, w_in, weight_sem.at[0]),
        pltpu.make_async_copy(w_out_hbm, w_out, weight_sem.at[1]),
    ]
    for copy in loads + weights:
        copy.start()

    barrier = pltpu.get_barrier_semaphore()
    for d in range(1, groups):
        pl.semaphore_signal(barrier, inc=1, device_id={"lon": lax.rem(g + d, groups)}, device_id_type=MESH)

    @pl.when(above)
    def _():
        pl.semaphore_signal(barrier, inc=1, device_id={"lat": t + 1}, device_id_type=MESH)

    @pl.when(below)
    def _():
        pl.semaphore_signal(barrier, inc=1, device_id={"lat": t - 1}, device_id_type=MESH)

    use_above = offsets[t] == t
    terms[...] = jnp.zeros_like(terms)
    for s in range(2):
        for k in range(count_k):
            terms[s, k:k + 1, 0:taps] = basis[k, t, s:s + 1, :]
    weight = jnp.concatenate([depth_weight[...], jnp.zeros((terms.shape[1] - count_k, channels), jnp.float32)], 0)
    both = [
        lax.dot_general(
            terms[s], weight, (((0,), (0,)), ((), ())),
            precision=lax.Precision.HIGHEST, preferred_element_type=jnp.float32,
        )
        for s in range(2)
    ]
    own_coef = jnp.where(use_above, both[0], both[1])
    nb_coef = jnp.where(use_above, both[1], both[0])
    for k in range(tiles):
        coef[0, k] = own_coef[:, k * LANES:(k + 1) * LANES]
        coef[1, k] = nb_coef[:, k * LANES:(k + 1) * LANES]

    length = lengths[g]
    for copy in loads:
        copy.wait()
    edge[:, 0:HALO, :] = raw[:, 0:HALO, :]
    for k in range(tiles):
        edge[k, HALO:2 * HALO, :] = raw[k, pl.ds(jnp.maximum(length - HALO, 0), HALO), :]

    pl.semaphore_wait(barrier, groups - 1 + above.astype(jnp.int32) + below.astype(jnp.int32))

    def edge_copy(d):
        return pltpu.make_async_remote_copy(
            src_ref=edge, dst_ref=peers.at[d], send_sem=edge_send.at[d], recv_sem=edge_recv.at[d],
            device_id={"lon": lax.rem(g + d, groups)}, device_id_type=MESH,
        )

    def row_copy(side, c):
        first = 0 if c == 0 else c * n + HALO
        last = cap if c == blocks - 1 else (c + 1) * n + HALO
        rows = pl.ds(first, last - first)
        return pltpu.make_async_remote_copy(
            src_ref=raw.at[:, rows, :], dst_ref=nb.at[side, :, rows, :],
            send_sem=row_send.at[side, c], recv_sem=row_recv.at[side, c],
            device_id={"lat": t + 1 - 2 * side}, device_id_type=MESH,
        )

    def halo_copy(side):
        return pltpu.make_async_remote_copy(
            src_ref=halo, dst_ref=nb_halo.at[side], send_sem=halo_send.at[side], recv_sem=halo_recv.at[side],
            device_id={"lat": t + 1 - 2 * side}, device_id_type=MESH,
        )

    def sends(act):
        for side, exists in ((0, above), (1, below)):
            pl.when(exists)(functools.partial(act, side))

    def receives(act):
        for side, exists in ((0, below), (1, above)):
            pl.when(exists)(functools.partial(act, side))

    for d in range(1, groups):
        edge_copy(d).start()
    sends(lambda side: row_copy(side, 0).start())
    for d in range(1, groups):
        edge_copy(d).wait_recv()

    steps = min(HALO, groups - 1)
    right = [(groups - 1 - q, lengths[lax.rem(g + 1 + q, groups)]) for q in range(steps)]
    left = [(1 + q, lengths[lax.rem(g + groups - 1 - q, groups)]) for q in range(steps)]
    for j in range(HALO):
        source, slot, passed = right[0][0], jnp.int32(j), jnp.int32(0)
        for q in range(1, steps):
            passed = passed + right[q - 1][1]
            source = jnp.where(passed <= j, right[q][0], source)
            slot = jnp.where(passed <= j, j - passed, slot)
        halo[:, HALO + j:HALO + j + 1, :] = peers[source, :, pl.ds(slot, 1), :]
        back = HALO - j
        source, row, passed = left[0][0], HALO + jnp.minimum(left[0][1], HALO) - back, jnp.int32(0)
        for q in range(1, steps):
            passed = passed + left[q - 1][1]
            reach = passed < back
            source = jnp.where(reach, left[q][0], source)
            row = jnp.where(reach, HALO + jnp.minimum(left[q][1], HALO) - (back - passed), row)
        halo[:, j:j + 1, :] = peers[source, :, pl.ds(jnp.maximum(row, 0), 1), :]

    sends(lambda side: halo_copy(side).start())
    for c in range(1, blocks):
        sends(lambda side: row_copy(side, c).start())

    def extend(target, values, tail_ref, first, last):
        def tile(k, carry):
            moved = tail_ref[k, pl.ds(cap + first - length, last - first), :]
            inside = first + lax.broadcasted_iota(jnp.int32, moved.shape, 0) < length
            target[k, HALO + first:HALO + last, :] = jnp.where(inside, values(k, first, last), moved)
            return carry

        lax.fori_loop(0, tiles, tile, 0)

    def extend_end(target, tail_ref):
        for k in range(tiles):
            target[k, HALO + cap:2 * HALO + cap, :] = tail_ref[k, pl.ds(cap + cap - length, HALO), :]

    def conv(source, which, k, start):
        total = None
        for shift in range(HALO):
            reach = n + HALO * ((taps - 1 - shift) // HALO)
            moved = source[k, start + shift:start + shift + reach, :]
            for tap in range(shift, taps, HALO):
                term = moved[tap - shift:tap - shift + n] * coef[which, k, tap:tap + 1, :]
                total = term if total is None else total + term
        return total

    tail[:, cap:cap + HALO, :] = halo[:, HALO:2 * HALO, :]
    ext[:, 0:HALO, :] = halo[:, 0:HALO, :]
    for c in range(blocks):
        extend(ext, lambda k, a, b: raw[k, a:b, :], tail, c * n, (c + 1) * n)
    extend_end(ext, tail)
    for c in range(blocks):
        def own_tile(k, carry):
            acc[k, c * n:(c + 1) * n, :] = raw[k, c * n:(c + 1) * n, :] + conv(ext, 0, k, c * n)
            return carry

        lax.fori_loop(0, tiles, own_tile, 0)

    receives(lambda side: halo_copy(side).wait_recv())
    for k in range(tiles):
        both_halos = jnp.where(use_above, nb_halo[1, k], nb_halo[0, k])
        ext_nb[k, 0:HALO, :] = both_halos[0:HALO]
        tail_nb[k, cap:cap + HALO, :] = both_halos[HALO:2 * HALO]
    for copy in weights:
        copy.wait()

    writes = []
    for c in range(blocks):
        receives(lambda side: row_copy(side, c).wait_recv())
        first = 0 if c == 0 else c * n + HALO
        last = cap if c == blocks - 1 else (c + 1) * n + HALO
        extend(ext_nb, lambda k, a, b: jnp.where(use_above, nb[1, k, a:b, :], nb[0, k, a:b, :]), tail_nb, first, last)
        if c == blocks - 1:
            extend_end(ext_nb, tail_nb)

        def nb_tile(k, squares):
            state = acc[k, c * n:(c + 1) * n, :] + conv(ext_nb, 1, k, c * n)
            st[k] = state
            return squares + state * state

        squares = lax.fori_loop(0, tiles, nb_tile, jnp.zeros((n, LANES), jnp.float32))
        scale = lax.rsqrt(jnp.sum(squares, axis=1, keepdims=True) * (1.0 / channels) + 1e-05)
        state = jnp.concatenate([st[k] for k in range(tiles)], axis=1)
        normed = (state * scale * gain[...]).astype(jnp.bfloat16)
        total = state + b_out[...]
        for h in range(0, hidden, hid_block):
            pre = jnp.dot(normed, w_in[:, h:h + hid_block], preferred_element_type=jnp.float32) + b_in[:, h:h + hid_block]
            active = (0.5 * pre * (1.0 + lax.erf(pre * SQRT_HALF))).astype(jnp.bfloat16)
            total = total + jnp.dot(active, w_out[h:h + hid_block, :], preferred_element_type=jnp.float32)
        inside = c * n + lax.broadcasted_iota(jnp.int32, total.shape, 0) < length
        out_buf[c * n:(c + 1) * n, :] = jnp.where(inside, total, 0.0)
        write = pltpu.make_async_copy(
            out_buf.at[pl.ds(c * n, n), :], out_hbm.at[0, pl.ds(c * n, n), :], out_sem.at[c]
        )
        write.start()
        writes.append(write)

    for d in range(1, groups):
        edge_copy(d).wait_send()
    sends(lambda side: halo_copy(side).wait_send())
    for c in range(blocks):
        sends(lambda side: row_copy(side, c).wait_send())
    for write in writes:
        write.wait()


def on_device(groups, lat_count, field, piece_lengths, offsets, basis, depth_weight, gain, w_in, b_in, w_out, b_out):
    rows_dev, slot_cap, channels = field.shape
    assert rows_dev == 1 and basis.shape[2] == 2 and basis.shape[3] == 2 * HALO + 1
    cap = round_up(slot_cap, 8)
    if cap != slot_cap:
        field = jnp.pad(field, ((0, 0), (0, cap - slot_cap), (0, 0)))
    tiles = channels // LANES
    hidden = w_in.shape[1]
    n = block_rows(cap, 120)
    blocks = cap // n
    hid_block = 256 if hidden % 256 == 0 else LANES
    taps = basis.shape[3]
    k_rows = round_up(basis.shape[0], 8)
    vmem = pl.BlockSpec(memory_space=pltpu.VMEM)
    smem = pl.BlockSpec(memory_space=pltpu.SMEM)
    hbm = pl.BlockSpec(memory_space=pl.ANY)
    f32 = jnp.float32
    out = pl.pallas_call(
        functools.partial(kernel, groups, lat_count, n, hid_block),
        out_shape=jax.ShapeDtypeStruct((1, cap, channels), f32),
        in_specs=[smem, smem, hbm, vmem, vmem, vmem, hbm, vmem, hbm, vmem],
        out_specs=hbm,
        scratch_shapes=[
            pltpu.VMEM((tiles, cap, LANES), f32),
            pltpu.VMEM((tiles, 2 * HALO, LANES), f32),
            pltpu.VMEM((groups, tiles, 2 * HALO, LANES), f32),
            pltpu.VMEM((tiles, 2 * HALO, LANES), f32),
            pltpu.VMEM((2, tiles, cap, LANES), f32),
            pltpu.VMEM((2, tiles, 2 * HALO, LANES), f32),
            pltpu.VMEM((tiles, cap + 2 * HALO, LANES), f32),
            pltpu.VMEM((tiles, cap + 2 * HALO, LANES), f32),
            pltpu.VMEM((tiles, 2 * cap + 2 * HALO, LANES), f32),
            pltpu.VMEM((tiles, 2 * cap + 2 * HALO, LANES), f32),
            pltpu.VMEM((2, k_rows, round_up(taps, 8)), f32),
            pltpu.VMEM((2, tiles, round_up(taps, 8), LANES), f32),
            pltpu.VMEM((tiles, cap, LANES), f32),
            pltpu.VMEM((tiles, n, LANES), f32),
            pltpu.VMEM((cap, channels), f32),
            pltpu.VMEM(w_in.shape, w_in.dtype),
            pltpu.VMEM(w_out.shape, w_out.dtype),
            pltpu.SemaphoreType.DMA((tiles,)),
            pltpu.SemaphoreType.DMA((2,)),
            pltpu.SemaphoreType.DMA((groups,)),
            pltpu.SemaphoreType.DMA((groups,)),
            pltpu.SemaphoreType.DMA((2,)),
            pltpu.SemaphoreType.DMA((2,)),
            pltpu.SemaphoreType.DMA((2, blocks)),
            pltpu.SemaphoreType.DMA((2, blocks)),
            pltpu.SemaphoreType.DMA((blocks,)),
        ],
        compiler_params=pltpu.CompilerParams(
            collective_id=0, has_side_effects=True, vmem_limit_bytes=40 * 1024 * 1024
        ),
        cost_estimate=pl.CostEstimate(flops=4 * cap * channels * hidden, bytes_accessed=6 * 1024 * 1024, transcendentals=0),
    )(
        piece_lengths, offsets, field, basis, depth_weight, gain.reshape(1, -1),
        w_in, b_in.reshape(1, -1), w_out, b_out.reshape(1, -1),
    )
    return out[:, :slot_cap, :]


def solution(mesh):
    placed = (P(("ens", "lat"), "lon", None), P(), P(), P(), P(), P(), P(), P(), P(), P())
    return jax.shard_map(
        functools.partial(on_device, mesh.shape["lon"], mesh.shape["lat"]),
        mesh=mesh,
        in_specs=placed,
        out_specs=P(("ens", "lat"), "lon", None),
        check_vma=False,
    )
```

```python
import functools
import jax
import jax.numpy as jnp
from jax import lax
from jax.experimental import pallas as pl
from jax.experimental.pallas import tpu as pltpu
from jax.sharding import PartitionSpec as P

LANES = 128
HALO = 8
MESH = pl.DeviceIdType.MESH
SQRT_HALF = 0.7071067811865476


def round_up(value, step):
    return -(-value // step) * step


def block_rows(total, most):
    return max(rows for rows in range(8, most + 1, 8) if total % rows == 0)


def kernel(
    groups, lat_count, n, hid_block,
    lengths_hbm, offsets_hbm, field, basis_hbm, depth_hbm, gain_hbm, w_in_hbm, b_in_hbm, w_out_hbm, b_out_hbm,
    out_hbm,
    lengths, offsets, basis, depth_weight, gain, b_in, b_out,
    raw, edge, peers, halo, nb, nb_halo, ext, ext_nb, tail, tail_nb, terms, coef, acc, st, out_buf, w_in, w_out,
    load_sem, small_sem, weight_sem, edge_send, edge_recv, halo_send, halo_recv, row_send, row_recv, out_sem,
):
    cap = raw.shape[1]
    tiles = raw.shape[0]
    channels = tiles * LANES
    taps = basis.shape[3]
    count_k = basis.shape[0]
    blocks = cap // n
    hidden = w_in.shape[1]
    g = lax.axis_index("lon")
    t = lax.axis_index("lat")
    above, below = t < lat_count - 1, t > 0

    loads = [
        pltpu.make_async_copy(field.at[0, :, pl.ds(k * LANES, LANES)], raw.at[k], load_sem.at[k])
        for k in range(tiles)
    ]
    weights = [
        pltpu.make_async_copy(w_in_hbm, w_in, weight_sem.at[0]),
        pltpu.make_async_copy(w_out_hbm, w_out, weight_sem.at[1]),
    ]
    pairs = [
        (lengths_hbm, lengths), (offsets_hbm, offsets), (basis_hbm, basis), (depth_hbm, depth_weight),
        (gain_hbm, gain.at[0]), (b_in_hbm, b_in.at[0]), (b_out_hbm, b_out.at[0]),
    ]
    smalls = [pltpu.make_async_copy(source, target, small_sem.at[i]) for i, (source, target) in enumerate(pairs)]
    for copy in loads + smalls + weights:
        copy.start()

    barrier = pltpu.get_barrier_semaphore()
    for d in range(1, groups):
        pl.semaphore_signal(barrier, inc=1, device_id={"lon": lax.rem(g + d, groups)}, device_id_type=MESH)

    @pl.when(above)
    def _():
        pl.semaphore_signal(barrier, inc=1, device_id={"lat": t + 1}, device_id_type=MESH)

    @pl.when(below)
    def _():
        pl.semaphore_signal(barrier, inc=1, device_id={"lat": t - 1}, device_id_type=MESH)

    for copy in smalls:
        copy.wait()
    use_above = offsets[t] == t
    terms[...] = jnp.zeros_like(terms)
    for s in range(2):
        for k in range(count_k):
            terms[s, k:k + 1, 0:taps] = basis[k, t, s:s + 1, :]
    weight = jnp.concatenate([depth_weight[...], jnp.zeros((terms.shape[1] - count_k, channels), jnp.float32)], 0)
    both = [
        lax.dot_general(
            terms[s], weight, (((0,), (0,)), ((), ())),
            precision=lax.Precision.HIGHEST, preferred_element_type=jnp.float32,
        )
        for s in range(2)
    ]
    own_coef = jnp.where(use_above, both[0], both[1])
    nb_coef = jnp.where(use_above, both[1], both[0])
    for k in range(tiles):
        coef[0, k] = own_coef[:, k * LANES:(k + 1) * LANES]
        coef[1, k] = nb_coef[:, k * LANES:(k + 1) * LANES]

    length = lengths[g]
    for copy in loads:
        copy.wait()
    edge[:, 0:HALO, :] = raw[:, 0:HALO, :]
    for k in range(tiles):
        edge[k, HALO:2 * HALO, :] = raw[k, pl.ds(jnp.maximum(length - HALO, 0), HALO), :]

    pl.semaphore_wait(barrier, groups - 1 + above.astype(jnp.int32) + below.astype(jnp.int32))

    def edge_copy(d):
        return pltpu.make_async_remote_copy(
            src_ref=edge, dst_ref=peers.at[d], send_sem=edge_send.at[d], recv_sem=edge_recv.at[d],
            device_id={"lon": lax.rem(g + d, groups)}, device_id_type=MESH,
        )

    def row_copy(side, c):
        first = 0 if c == 0 else c * n + HALO
        last = cap if c == blocks - 1 else (c + 1) * n + HALO
        rows = pl.ds(first, last - first)
        return pltpu.make_async_remote_copy(
            src_ref=raw.at[:, rows, :], dst_ref=nb.at[side, :, rows, :],
            send_sem=row_send.at[side, c], recv_sem=row_recv.at[side, c],
            device_id={"lat": t + 1 - 2 * side}, device_id_type=MESH,
        )

    def halo_copy(side):
        return pltpu.make_async_remote_copy(
            src_ref=halo, dst_ref=nb_halo.at[side], send_sem=halo_send.at[side], recv_sem=halo_recv.at[side],
            device_id={"lat": t + 1 - 2 * side}, device_id_type=MESH,
        )

    odd = lax.rem(t, 2) == 1

    def sends(act):
        for side, exists in ((0, above & odd), (1, below & ~odd), (0, above & ~odd), (1, below & odd)):
            pl.when(exists)(functools.partial(act, side))

    def receives(act):
        for side, exists in ((0, below), (1, above)):
            pl.when(exists)(functools.partial(act, side))

    for d in range(1, groups):
        edge_copy(d).start()
    sends(lambda side: row_copy(side, 0).start())
    for d in range(1, groups):
        edge_copy(d).wait_recv()

    steps = min(HALO, groups - 1)
    right = [(groups - 1 - q, lengths[lax.rem(g + 1 + q, groups)]) for q in range(steps)]
    left = [(1 + q, lengths[lax.rem(g + groups - 1 - q, groups)]) for q in range(steps)]
    for j in range(HALO):
        source, slot, passed = right[0][0], jnp.int32(j), jnp.int32(0)
        for q in range(1, steps):
            passed = passed + right[q - 1][1]
            source = jnp.where(passed <= j, right[q][0], source)
            slot = jnp.where(passed <= j, j - passed, slot)
        halo[:, HALO + j:HALO + j + 1, :] = peers[source, :, pl.ds(slot, 1), :]
        back = HALO - j
        source, row, passed = left[0][0], HALO + jnp.minimum(left[0][1], HALO) - back, jnp.int32(0)
        for q in range(1, steps):
            passed = passed + left[q - 1][1]
            reach = passed < back
            source = jnp.where(reach, left[q][0], source)
            row = jnp.where(reach, HALO + jnp.minimum(left[q][1], HALO) - (back - passed), row)
        halo[:, j:j + 1, :] = peers[source, :, pl.ds(jnp.maximum(row, 0), 1), :]

    sends(lambda side: halo_copy(side).start())
    for c in range(1, blocks):
        sends(lambda side: row_copy(side, c).start())

    def extend(target, values, tail_ref, first, last):
        def tile(k, carry):
            moved = tail_ref[k, pl.ds(cap + first - length, last - first), :]
            inside = first + lax.broadcasted_iota(jnp.int32, moved.shape, 0) < length
            target[k, HALO + first:HALO + last, :] = jnp.where(inside, values(k, first, last), moved)
            return carry

        lax.fori_loop(0, tiles, tile, 0)

    def extend_end(target, tail_ref):
        for k in range(tiles):
            target[k, HALO + cap:2 * HALO + cap, :] = tail_ref[k, pl.ds(cap + cap - length, HALO), :]

    def conv(source, which, k, start):
        total = None
        for shift in range(HALO):
            reach = n + HALO * ((taps - 1 - shift) // HALO)
            moved = source[k, start + shift:start + shift + reach, :]
            for tap in range(shift, taps, HALO):
                term = moved[tap - shift:tap - shift + n] * coef[which, k, tap:tap + 1, :]
                total = term if total is None else total + term
        return total

    tail[:, cap:cap + HALO, :] = halo[:, HALO:2 * HALO, :]
    ext[:, 0:HALO, :] = halo[:, 0:HALO, :]
    for c in range(blocks):
        extend(ext, lambda k, a, b: raw[k, a:b, :], tail, c * n, (c + 1) * n)
    extend_end(ext, tail)
    for c in range(blocks):
        def own_tile(k, carry):
            acc[k, c * n:(c + 1) * n, :] = raw[k, c * n:(c + 1) * n, :] + conv(ext, 0, k, c * n)
            return carry

        lax.fori_loop(0, tiles, own_tile, 0)

    receives(lambda side: halo_copy(side).wait_recv())
    for k in range(tiles):
        both_halos = jnp.where(use_above, nb_halo[1, k], nb_halo[0, k])
        ext_nb[k, 0:HALO, :] = both_halos[0:HALO]
        tail_nb[k, cap:cap + HALO, :] = both_halos[HALO:2 * HALO]
    for copy in weights:
        copy.wait()

    writes = []
    for c in range(blocks):
        receives(lambda side: row_copy(side, c).wait_recv())
        first = 0 if c == 0 else c * n + HALO
        last = cap if c == blocks - 1 else (c + 1) * n + HALO
        extend(ext_nb, lambda k, a, b: jnp.where(use_above, nb[1, k, a:b, :], nb[0, k, a:b, :]), tail_nb, first, last)
        if c == blocks - 1:
            extend_end(ext_nb, tail_nb)

        def nb_tile(k, squares):
            state = acc[k, c * n:(c + 1) * n, :] + conv(ext_nb, 1, k, c * n)
            st[k] = state
            return squares + state * state

        squares = lax.fori_loop(0, tiles, nb_tile, jnp.zeros((n, LANES), jnp.float32))
        scale = lax.rsqrt(jnp.sum(squares, axis=1, keepdims=True) * (1.0 / channels) + 1e-05)
        state = jnp.concatenate([st[k] for k in range(tiles)], axis=1)
        normed = (state * scale * gain[...]).astype(jnp.bfloat16)
        total = state + b_out[...]
        for h in range(0, hidden, hid_block):
            pre = jnp.dot(normed, w_in[:, h:h + hid_block], preferred_element_type=jnp.float32) + b_in[:, h:h + hid_block]
            active = (0.5 * pre * (1.0 + lax.erf(pre * SQRT_HALF))).astype(jnp.bfloat16)
            total = total + jnp.dot(active, w_out[h:h + hid_block, :], preferred_element_type=jnp.float32)
        inside = c * n + lax.broadcasted_iota(jnp.int32, total.shape, 0) < length
        out_buf[c * n:(c + 1) * n, :] = jnp.where(inside, total, 0.0)
        write = pltpu.make_async_copy(
            out_buf.at[pl.ds(c * n, n), :], out_hbm.at[0, pl.ds(c * n, n), :], out_sem.at[c]
        )
        write.start()
        writes.append(write)

    for d in range(1, groups):
        edge_copy(d).wait_send()
    sends(lambda side: halo_copy(side).wait_send())
    for c in range(blocks):
        sends(lambda side: row_copy(side, c).wait_send())
    for write in writes:
        write.wait()


def on_device(groups, lat_count, field, piece_lengths, offsets, basis, depth_weight, gain, w_in, b_in, w_out, b_out):
    rows_dev, slot_cap, channels = field.shape
    assert rows_dev == 1 and basis.shape[2] == 2 and basis.shape[3] == 2 * HALO + 1
    cap = round_up(slot_cap, 8)
    if cap != slot_cap:
        field = jnp.pad(field, ((0, 0), (0, cap - slot_cap), (0, 0)))
    tiles = channels // LANES
    hidden = w_in.shape[1]
    n = block_rows(cap, 72)
    blocks = cap // n
    hid_block = 256 if hidden % 256 == 0 else LANES
    taps = basis.shape[3]
    k_rows = round_up(basis.shape[0], 8)
    hbm = pl.BlockSpec(memory_space=pltpu.HBM)
    f32 = jnp.float32
    out = pl.pallas_call(
        functools.partial(kernel, groups, lat_count, n, hid_block),
        out_shape=jax.ShapeDtypeStruct((1, cap, channels), f32),
        in_specs=[hbm] * 10,
        out_specs=pl.BlockSpec(memory_space=pl.ANY),
        scratch_shapes=[
            pltpu.SMEM(piece_lengths.shape, jnp.int32),
            pltpu.SMEM(offsets.shape, jnp.int32),
            pltpu.VMEM(basis.shape, f32),
            pltpu.VMEM(depth_weight.shape, f32),
            pltpu.VMEM((1, channels), f32),
            pltpu.VMEM((1, hidden), f32),
            pltpu.VMEM((1, channels), f32),
            pltpu.VMEM((tiles, cap, LANES), f32),
            pltpu.VMEM((tiles, 2 * HALO, LANES), f32),
            pltpu.VMEM((groups, tiles, 2 * HALO, LANES), f32),
            pltpu.VMEM((tiles, 2 * HALO, LANES), f32),
            pltpu.VMEM((2, tiles, cap, LANES), f32),
            pltpu.VMEM((2, tiles, 2 * HALO, LANES), f32),
            pltpu.VMEM((tiles, cap + 2 * HALO, LANES), f32),
            pltpu.VMEM((tiles, cap + 2 * HALO, LANES), f32),
            pltpu.VMEM((tiles, 2 * cap + 2 * HALO, LANES), f32),
            pltpu.VMEM((tiles, 2 * cap + 2 * HALO, LANES), f32),
            pltpu.VMEM((2, k_rows, round_up(taps, 8)), f32),
            pltpu.VMEM((2, tiles, round_up(taps, 8), LANES), f32),
            pltpu.VMEM((tiles, cap, LANES), f32),
            pltpu.VMEM((tiles, n, LANES), f32),
            pltpu.VMEM((cap, channels), f32),
            pltpu.VMEM(w_in.shape, w_in.dtype),
            pltpu.VMEM(w_out.shape, w_out.dtype),
            pltpu.SemaphoreType.DMA((tiles,)),
            pltpu.SemaphoreType.DMA((7,)),
            pltpu.SemaphoreType.DMA((2,)),
            pltpu.SemaphoreType.DMA((groups,)),
            pltpu.SemaphoreType.DMA((groups,)),
            pltpu.SemaphoreType.DMA((2,)),
            pltpu.SemaphoreType.DMA((2,)),
            pltpu.SemaphoreType.DMA((2, blocks)),
            pltpu.SemaphoreType.DMA((2, blocks)),
            pltpu.SemaphoreType.DMA((blocks,)),
        ],
        compiler_params=pltpu.CompilerParams(
            collective_id=0, has_side_effects=True, vmem_limit_bytes=64 * 1024 * 1024
        ),
        cost_estimate=pl.CostEstimate(flops=4 * cap * channels * hidden, bytes_accessed=6 * 1024 * 1024, transcendentals=0),
    )(
        piece_lengths, offsets, field, basis, depth_weight, gain, w_in, b_in, w_out, b_out,
    )
    return out[:, :slot_cap, :]


def solution(mesh):
    placed = (P(("ens", "lat"), "lon", None), P(), P(), P(), P(), P(), P(), P(), P(), P())
    return jax.shard_map(
        functools.partial(on_device, mesh.shape["lon"], mesh.shape["lat"]),
        mesh=mesh,
        in_specs=placed,
        out_specs=P(("ens", "lat"), "lon", None),
        check_vma=False,
    )
```

```python
import functools
import jax
import jax.numpy as jnp
from jax import lax
from jax.experimental import pallas as pl
from jax.experimental.pallas import tpu as pltpu
from jax.sharding import PartitionSpec as P

LANES = 128
HALO = 8
MESH = pl.DeviceIdType.MESH
SQRT_HALF = 0.7071067811865476


def round_up(value, step):
    return -(-value // step) * step


def block_rows(total, most):
    return max(rows for rows in range(8, most + 1, 8) if total % rows == 0)


def kernel(
    groups, lat_count, n, hid_block,
    lengths_hbm, offsets_hbm, field, basis_hbm, depth_hbm, gain_hbm, w_in_hbm, b_in_hbm, w_out_hbm, b_out_hbm,
    out_hbm,
    lengths, offsets, basis, depth_weight, gain, b_in, b_out,
    raw, edge, peers, halo, nb, nb_halo, ext, ext_nb, tail, terms, coef, acc, st, out_buf, w_in, w_out,
    load_sem, small_sem, weight_sem, edge_send, edge_recv, halo_send, halo_recv, row_send, row_recv, out_sem,
):
    cap = raw.shape[1]
    tiles = raw.shape[0]
    channels = tiles * LANES
    taps = basis.shape[3]
    count_k = basis.shape[0]
    blocks = cap // n
    hidden = w_in.shape[1]
    g = lax.axis_index("lon")
    t = lax.axis_index("lat")
    above, below = t < lat_count - 1, t > 0

    loads = [
        pltpu.make_async_copy(field.at[0, :, pl.ds(k * LANES, LANES)], raw.at[k], load_sem.at[k])
        for k in range(tiles)
    ]
    weights = [
        pltpu.make_async_copy(w_in_hbm, w_in, weight_sem.at[0]),
        pltpu.make_async_copy(w_out_hbm, w_out, weight_sem.at[1]),
    ]
    pairs = [
        (lengths_hbm, lengths), (offsets_hbm, offsets), (basis_hbm, basis), (depth_hbm, depth_weight),
        (gain_hbm, gain.at[0]), (b_in_hbm, b_in.at[0]), (b_out_hbm, b_out.at[0]),
    ]
    smalls = [pltpu.make_async_copy(source, target, small_sem.at[i]) for i, (source, target) in enumerate(pairs)]
    for copy in loads + smalls + weights:
        copy.start()

    barrier = pltpu.get_barrier_semaphore()

    @pl.when(above)
    def _():
        pl.semaphore_signal(barrier, inc=1, device_id={"lat": t + 1}, device_id_type=MESH)

    @pl.when(below)
    def _():
        pl.semaphore_signal(barrier, inc=1, device_id={"lat": t - 1}, device_id_type=MESH)

    for d in range(1, groups):
        pl.semaphore_signal(barrier, inc=1, device_id={"lon": lax.rem(g + d, groups)}, device_id_type=MESH)

    tail[...] = jnp.zeros_like(tail)
    for target in (ext, ext_nb):
        target[:, 0:HALO, :] = jnp.zeros((tiles, HALO, LANES), jnp.float32)
        target[:, cap + HALO:cap + 2 * HALO, :] = jnp.zeros((tiles, HALO, LANES), jnp.float32)

    smalls[0].wait()
    length = lengths[g]
    for copy in loads:
        copy.wait()
    edge[:, 0:HALO, :] = raw[:, 0:HALO, :]
    for k in range(tiles):
        edge[k, HALO:2 * HALO, :] = raw[k, pl.ds(jnp.maximum(length - HALO, 0), HALO), :]

    pl.semaphore_wait(barrier, groups - 1 + above.astype(jnp.int32) + below.astype(jnp.int32))

    def edge_copy(d):
        return pltpu.make_async_remote_copy(
            src_ref=edge, dst_ref=peers.at[d], send_sem=edge_send.at[d], recv_sem=edge_recv.at[d],
            device_id={"lon": lax.rem(g + d, groups)}, device_id_type=MESH,
        )

    def span(c):
        first = 0 if c == 0 else c * n + HALO
        last = cap if c == blocks - 1 else (c + 1) * n + HALO
        return first, last

    def row_copy(side, c):
        first, last = span(c)
        rows = pl.ds(first, last - first)
        return pltpu.make_async_remote_copy(
            src_ref=raw.at[:, rows, :], dst_ref=nb.at[side, :, rows, :],
            send_sem=row_send.at[side, c], recv_sem=row_recv.at[side, c],
            device_id={"lat": t + 1 - 2 * side}, device_id_type=MESH,
        )

    def halo_copy(side):
        return pltpu.make_async_remote_copy(
            src_ref=halo, dst_ref=nb_halo.at[side], send_sem=halo_send.at[side], recv_sem=halo_recv.at[side],
            device_id={"lat": t + 1 - 2 * side}, device_id_type=MESH,
        )

    odd = lax.rem(t, 2) == 1

    def sends(act):
        for side, exists in ((0, above & odd), (1, below & ~odd), (0, above & ~odd), (1, below & odd)):
            pl.when(exists)(functools.partial(act, side))

    def receives(act):
        for side, exists in ((0, below), (1, above)):
            pl.when(exists)(functools.partial(act, side))

    for d in range(1, groups):
        edge_copy(d).start()
    sends(lambda side: row_copy(side, 0).start())

    for copy in smalls[1:]:
        copy.wait()
    use_above = offsets[t] == t
    terms[...] = jnp.zeros_like(terms)
    for s in range(2):
        for k in range(count_k):
            terms[s, k:k + 1, 0:taps] = basis[k, t, s:s + 1, :]
    weight = jnp.concatenate([depth_weight[...], jnp.zeros((terms.shape[1] - count_k, channels), jnp.float32)], 0)
    both = [
        lax.dot_general(
            terms[s], weight, (((0,), (0,)), ((), ())),
            precision=lax.Precision.HIGHEST, preferred_element_type=jnp.float32,
        )
        for s in range(2)
    ]
    own_coef = jnp.where(use_above, both[0], both[1])
    nb_coef = jnp.where(use_above, both[1], both[0])
    for k in range(tiles):
        coef[0, k] = own_coef[:, k * LANES:(k + 1) * LANES]
        coef[1, k] = nb_coef[:, k * LANES:(k + 1) * LANES]

    def conv(source, which, k, start):
        total = None
        for shift in range(HALO):
            reach = n + HALO * ((taps - 1 - shift) // HALO)
            moved = source[k, start + shift:start + shift + reach, :]
            for tap in range(shift, taps, HALO):
                term = moved[tap - shift:tap - shift + n] * coef[which, k, tap:tap + 1, :]
                total = term if total is None else total + term
        return total

    def extend(target, values, c):
        first, last = span(c)

        def tile(k, carry):
            inside = first + lax.broadcasted_iota(jnp.int32, (last - first, LANES), 0) < length
            target[k, HALO + first:HALO + last, :] = jnp.where(inside, values(k, first, last), 0.0)
            return carry

        lax.fori_loop(0, tiles, tile, 0)

    def own_block(c):
        def own_tile(k, carry):
            acc[k, c * n:(c + 1) * n, :] = raw[k, c * n:(c + 1) * n, :] + conv(ext, 0, k, c * n)
            return carry

        lax.fori_loop(0, tiles, own_tile, 0)

    for c in range(blocks):
        extend(ext, lambda k, a, b: raw[k, a:b, :], c)
    own_block(0)

    for d in range(1, groups):
        edge_copy(d).wait_recv()
    steps = min(HALO, groups - 1)
    right = [(groups - 1 - q, lengths[lax.rem(g + 1 + q, groups)]) for q in range(steps)]
    left = [(1 + q, lengths[lax.rem(g + groups - 1 - q, groups)]) for q in range(steps)]
    for j in range(HALO):
        source, slot, passed = right[0][0], jnp.int32(j), jnp.int32(0)
        for q in range(1, steps):
            passed = passed + right[q - 1][1]
            source = jnp.where(passed <= j, right[q][0], source)
            slot = jnp.where(passed <= j, j - passed, slot)
        halo[:, HALO + j:HALO + j + 1, :] = peers[source, :, pl.ds(slot, 1), :]
        back = HALO - j
        source, row, passed = left[0][0], HALO + jnp.minimum(left[0][1], HALO) - back, jnp.int32(0)
        for q in range(1, steps):
            passed = passed + left[q - 1][1]
            reach = passed < back
            source = jnp.where(reach, left[q][0], source)
            row = jnp.where(reach, HALO + jnp.minimum(left[q][1], HALO) - (back - passed), row)
        halo[:, j:j + 1, :] = peers[source, :, pl.ds(jnp.maximum(row, 0), 1), :]

    sends(lambda side: halo_copy(side).start())
    for c in range(1, blocks):
        sends(lambda side: row_copy(side, c).start())
    for c in range(1, blocks):
        own_block(c)

    receives(lambda side: halo_copy(side).wait_recv())
    around = jnp.zeros((2 * HALO, LANES), jnp.float32)
    for k in range(tiles):
        near = jnp.where(use_above, nb_halo[1, k], nb_halo[0, k])
        from_left, from_right = None, None
        for which, values in ((0, halo[k]), (1, near)):
            lefts = jnp.concatenate([values[0:HALO], around], axis=0)
            rights = jnp.concatenate([around, values[HALO:2 * HALO]], axis=0)
            for tap in range(taps):
                factor = coef[which, k, tap:tap + 1, :]
                if tap < HALO:
                    term = lefts[tap:tap + HALO] * factor
                    from_left = term if from_left is None else from_left + term
                if tap > HALO:
                    term = rights[tap:tap + HALO] * factor
                    from_right = term if from_right is None else from_right + term
        acc[k, 0:HALO, :] += from_left
        tail[k, cap - HALO:cap, :] = from_right
    for copy in weights:
        copy.wait()

    writes = []
    for c in range(blocks):
        receives(lambda side: row_copy(side, c).wait_recv())
        extend(ext_nb, lambda k, a, b: jnp.where(use_above, nb[1, k, a:b, :], nb[0, k, a:b, :]), c)

        def nb_tile(k, squares):
            state = acc[k, c * n:(c + 1) * n, :] + conv(ext_nb, 1, k, c * n) + tail[k, pl.ds(cap + c * n - length, n), :]
            st[k] = state
            return squares + state * state

        squares = lax.fori_loop(0, tiles, nb_tile, jnp.zeros((n, LANES), jnp.float32))
        scale = lax.rsqrt(jnp.sum(squares, axis=1, keepdims=True) * (1.0 / channels) + 1e-05)
        state = jnp.concatenate([st[k] for k in range(tiles)], axis=1)
        normed = (state * scale * gain[...]).astype(jnp.bfloat16)
        total = state + b_out[...]
        for h in range(0, hidden, hid_block):
            pre = jnp.dot(normed, w_in[:, h:h + hid_block], preferred_element_type=jnp.float32) + b_in[:, h:h + hid_block]
            active = (0.5 * pre * (1.0 + lax.erf(pre * SQRT_HALF))).astype(jnp.bfloat16)
            total = total + jnp.dot(active, w_out[h:h + hid_block, :], preferred_element_type=jnp.float32)
        inside = c * n + lax.broadcasted_iota(jnp.int32, total.shape, 0) < length
        out_buf[c * n:(c + 1) * n, :] = jnp.where(inside, total, 0.0)
        write = pltpu.make_async_copy(
            out_buf.at[pl.ds(c * n, n), :], out_hbm.at[0, pl.ds(c * n, n), :], out_sem.at[c]
        )
        write.start()
        writes.append(write)

    for d in range(1, groups):
        edge_copy(d).wait_send()
    sends(lambda side: halo_copy(side).wait_send())
    for c in range(blocks):
        sends(lambda side: row_copy(side, c).wait_send())
    for write in writes:
        write.wait()


def on_device(groups, lat_count, field, piece_lengths, offsets, basis, depth_weight, gain, w_in, b_in, w_out, b_out):
    rows_dev, slot_cap, channels = field.shape
    assert rows_dev == 1 and basis.shape[2] == 2 and basis.shape[3] == 2 * HALO + 1
    cap = round_up(slot_cap, 8)
    if cap != slot_cap:
        field = jnp.pad(field, ((0, 0), (0, cap - slot_cap), (0, 0)))
    tiles = channels // LANES
    hidden = w_in.shape[1]
    n = block_rows(cap, 120)
    blocks = cap // n
    hid_block = 256 if hidden % 256 == 0 else LANES
    taps = basis.shape[3]
    k_rows = round_up(basis.shape[0], 8)
    hbm = pl.BlockSpec(memory_space=pltpu.HBM)
    f32 = jnp.float32
    out = pl.pallas_call(
        functools.partial(kernel, groups, lat_count, n, hid_block),
        out_shape=jax.ShapeDtypeStruct((1, cap, channels), f32),
        in_specs=[hbm] * 10,
        out_specs=pl.BlockSpec(memory_space=pl.ANY),
        scratch_shapes=[
            pltpu.SMEM(piece_lengths.shape, jnp.int32),
            pltpu.SMEM(offsets.shape, jnp.int32),
            pltpu.VMEM(basis.shape, f32),
            pltpu.VMEM(depth_weight.shape, f32),
            pltpu.VMEM((1, channels), f32),
            pltpu.VMEM((1, hidden), f32),
            pltpu.VMEM((1, channels), f32),
            pltpu.VMEM((tiles, cap, LANES), f32),
            pltpu.VMEM((tiles, 2 * HALO, LANES), f32),
            pltpu.VMEM((groups, tiles, 2 * HALO, LANES), f32),
            pltpu.VMEM((tiles, 2 * HALO, LANES), f32),
            pltpu.VMEM((2, tiles, cap, LANES), f32),
            pltpu.VMEM((2, tiles, 2 * HALO, LANES), f32),
            pltpu.VMEM((tiles, cap + 2 * HALO, LANES), f32),
            pltpu.VMEM((tiles, cap + 2 * HALO, LANES), f32),
            pltpu.VMEM((tiles, 2 * cap + 2 * HALO, LANES), f32),
            pltpu.VMEM((2, k_rows, round_up(taps, 8)), f32),
            pltpu.VMEM((2, tiles, round_up(taps, 8), LANES), f32),
            pltpu.VMEM((tiles, cap, LANES), f32),
            pltpu.VMEM((tiles, n, LANES), f32),
            pltpu.VMEM((cap, channels), f32),
            pltpu.VMEM(w_in.shape, w_in.dtype),
            pltpu.VMEM(w_out.shape, w_out.dtype),
            pltpu.SemaphoreType.DMA((tiles,)),
            pltpu.SemaphoreType.DMA((7,)),
            pltpu.SemaphoreType.DMA((2,)),
            pltpu.SemaphoreType.DMA((groups,)),
            pltpu.SemaphoreType.DMA((groups,)),
            pltpu.SemaphoreType.DMA((2,)),
            pltpu.SemaphoreType.DMA((2,)),
            pltpu.SemaphoreType.DMA((2, blocks)),
            pltpu.SemaphoreType.DMA((2, blocks)),
            pltpu.SemaphoreType.DMA((blocks,)),
        ],
        compiler_params=pltpu.CompilerParams(
            collective_id=0, has_side_effects=True, vmem_limit_bytes=63 * 1024 * 1024
        ),
        cost_estimate=pl.CostEstimate(flops=4 * cap * channels * hidden, bytes_accessed=6 * 1024 * 1024, transcendentals=0),
    )(
        piece_lengths, offsets, field, basis, depth_weight, gain, w_in, b_in, w_out, b_out,
    )
    return out[:, :slot_cap, :]


def solution(mesh):
    placed = (P(("ens", "lat"), "lon", None), P(), P(), P(), P(), P(), P(), P(), P(), P())
    return jax.shard_map(
        functools.partial(on_device, mesh.shape["lon"], mesh.shape["lat"]),
        mesh=mesh,
        in_specs=placed,
        out_specs=P(("ens", "lat"), "lon", None),
        check_vma=False,
    )
```

```python
import functools
import jax
import jax.numpy as jnp
from jax import lax
from jax.experimental import pallas as pl
from jax.experimental.pallas import tpu as pltpu
from jax.sharding import PartitionSpec as P

LANES = 128
HALO = 8
MESH = pl.DeviceIdType.MESH
SQRT_HALF = 0.7071067811865476


def round_up(value, step):
    return -(-value // step) * step


def block_rows(total, most):
    return max(rows for rows in range(8, most + 1, 8) if total % rows == 0)


def kernel(
    groups, lat_count, n, hid_block,
    lengths_hbm, offsets_hbm, field, basis_hbm, depth_hbm, gain_hbm, w_in_hbm, b_in_hbm, w_out_hbm, b_out_hbm,
    out_hbm,
    lengths, offsets, basis, depth_weight, gain, b_in, b_out,
    raw, edge, peers, halo, nb, nb_halo, ext, ext_nb, tail, terms, coef, acc, st, out_buf, w_in, w_out,
    load_sem, small_sem, weight_sem, edge_send, edge_recv, halo_send, halo_recv, row_send, row_recv, pass_send, out_sem,
):
    cap = raw.shape[1]
    tiles = raw.shape[0]
    channels = tiles * LANES
    taps = basis.shape[3]
    count_k = basis.shape[0]
    blocks = cap // n
    hidden = w_in.shape[1]
    g = lax.axis_index("lon")
    t = lax.axis_index("lat")
    above, below = t < lat_count - 1, t > 0

    loads = [
        pltpu.make_async_copy(field.at[0, :, pl.ds(k * LANES, LANES)], raw.at[k], load_sem.at[k])
        for k in range(tiles)
    ]
    weights = [
        pltpu.make_async_copy(w_in_hbm, w_in, weight_sem.at[0]),
        pltpu.make_async_copy(w_out_hbm, w_out, weight_sem.at[1]),
    ]
    pairs = [
        (lengths_hbm, lengths), (offsets_hbm, offsets), (basis_hbm, basis), (depth_hbm, depth_weight),
        (gain_hbm, gain.at[0]), (b_in_hbm, b_in.at[0]), (b_out_hbm, b_out.at[0]),
    ]
    smalls = [pltpu.make_async_copy(source, target, small_sem.at[i]) for i, (source, target) in enumerate(pairs)]
    for copy in loads + smalls + weights:
        copy.start()

    barrier = pltpu.get_barrier_semaphore()

    @pl.when(above)
    def _():
        pl.semaphore_signal(barrier, inc=1, device_id={"lat": t + 1}, device_id_type=MESH)

    @pl.when(below)
    def _():
        pl.semaphore_signal(barrier, inc=1, device_id={"lat": t - 1}, device_id_type=MESH)

    @pl.when(t + 2 < lat_count)
    def _():
        pl.semaphore_signal(barrier, inc=1, device_id={"lat": t + 2}, device_id_type=MESH)

    @pl.when(t >= 2)
    def _():
        pl.semaphore_signal(barrier, inc=1, device_id={"lat": t - 2}, device_id_type=MESH)

    for d in range(1, groups):
        pl.semaphore_signal(barrier, inc=1, device_id={"lon": lax.rem(g + d, groups)}, device_id_type=MESH)

    tail[...] = jnp.zeros_like(tail)
    for target in (ext, ext_nb):
        target[:, 0:HALO, :] = jnp.zeros((tiles, HALO, LANES), jnp.float32)
        target[:, cap + HALO:cap + 2 * HALO, :] = jnp.zeros((tiles, HALO, LANES), jnp.float32)

    smalls[0].wait()
    length = lengths[g]
    for copy in loads:
        copy.wait()
    edge[:, 0:HALO, :] = raw[:, 0:HALO, :]
    for k in range(tiles):
        edge[k, HALO:2 * HALO, :] = raw[k, pl.ds(jnp.maximum(length - HALO, 0), HALO), :]

    greeted = [above, below, t + 2 < lat_count, t >= 2]
    pl.semaphore_wait(barrier, groups - 1 + sum(near.astype(jnp.int32) for near in greeted))

    def edge_copy(d):
        return pltpu.make_async_remote_copy(
            src_ref=edge, dst_ref=peers.at[d], send_sem=edge_send.at[d], recv_sem=edge_recv.at[d],
            device_id={"lon": lax.rem(g + d, groups)}, device_id_type=MESH,
        )

    def span(c):
        first = 0 if c == 0 else c * n + HALO
        last = cap if c == blocks - 1 else (c + 1) * n + HALO
        return first, last

    def half(c, h):
        first, last = span(c)
        middle = first + round_up((last - first) // 2, 8)
        return pl.ds(first, middle - first) if h == 0 else pl.ds(middle, last - middle)

    def row_copy(side, c, h):
        return pltpu.make_async_remote_copy(
            src_ref=raw.at[:, half(c, h), :], dst_ref=nb.at[side, :, half(c, h), :],
            send_sem=row_send.at[side, c, h], recv_sem=row_recv.at[side, c, h],
            device_id={"lat": t + 1 - 2 * side}, device_id_type=MESH,
        )

    def pass_copy(side, c):
        return pltpu.make_async_remote_copy(
            src_ref=nb.at[1 - side, :, half(c, 1), :], dst_ref=nb.at[side, :, half(c, 1), :],
            send_sem=pass_send.at[c], recv_sem=row_recv.at[side, c, 1],
            device_id={"lat": t + 2 - 4 * side}, device_id_type=MESH,
        )

    def halo_copy(side):
        return pltpu.make_async_remote_copy(
            src_ref=halo, dst_ref=nb_halo.at[side], send_sem=halo_send.at[side], recv_sem=halo_recv.at[side],
            device_id={"lat": t + 1 - 2 * side}, device_id_type=MESH,
        )

    odd = lax.rem(t, 2) == 1

    def crossing(act):
        pl.when(above & odd)(functools.partial(act, 0))
        pl.when(below & ~odd)(functools.partial(act, 1))

    def crossed(act):
        pl.when(above & odd)(functools.partial(act, 1))
        pl.when(below & ~odd)(functools.partial(act, 0))

    def to_mate(act):
        pl.when(~odd)(functools.partial(act, 0))
        pl.when(odd)(functools.partial(act, 1))

    def from_mate(act):
        pl.when(~odd)(functools.partial(act, 1))
        pl.when(odd)(functools.partial(act, 0))

    def passing(act):
        pl.when(~odd & (t + 2 < lat_count))(functools.partial(act, 0))
        pl.when(odd & (t >= 2))(functools.partial(act, 1))

    def send_block(c):
        crossing(lambda side: row_copy(side, c, 0).start())
        to_mate(lambda side: row_copy(side, c, 1).start())
        to_mate(lambda side: row_copy(side, c, 0).start())

    def pass_block(c):
        from_mate(lambda side: row_copy(side, c, 1).wait_recv())
        passing(lambda side: pass_copy(side, c).start())

    for d in range(1, groups):
        edge_copy(d).start()
    for c in range(max(1, blocks - 1)):
        send_block(c)

    for copy in smalls[1:]:
        copy.wait()
    use_above = offsets[t] == t
    terms[...] = jnp.zeros_like(terms)
    for s in range(2):
        for k in range(count_k):
            terms[s, k:k + 1, 0:taps] = basis[k, t, s:s + 1, :]
    weight = jnp.concatenate([depth_weight[...], jnp.zeros((terms.shape[1] - count_k, channels), jnp.float32)], 0)
    both = [
        lax.dot_general(
            terms[s], weight, (((0,), (0,)), ((), ())),
            precision=lax.Precision.HIGHEST, preferred_element_type=jnp.float32,
        )
        for s in range(2)
    ]
    own_coef = jnp.where(use_above, both[0], both[1])
    nb_coef = jnp.where(use_above, both[1], both[0])
    for k in range(tiles):
        coef[0, k] = own_coef[:, k * LANES:(k + 1) * LANES]
        coef[1, k] = nb_coef[:, k * LANES:(k + 1) * LANES]

    def conv(source, which, k, start):
        total = None
        for shift in range(HALO):
            reach = n + HALO * ((taps - 1 - shift) // HALO)
            moved = source[k, start + shift:start + shift + reach, :]
            for tap in range(shift, taps, HALO):
                term = moved[tap - shift:tap - shift + n] * coef[which, k, tap:tap + 1, :]
                total = term if total is None else total + term
        return total

    def extend(target, values, c):
        first, last = span(c)

        def tile(k, carry):
            inside = first + lax.broadcasted_iota(jnp.int32, (last - first, LANES), 0) < length
            target[k, HALO + first:HALO + last, :] = jnp.where(inside, values(k, first, last), 0.0)
            return carry

        lax.fori_loop(0, tiles, tile, 0)

    def own_block(c):
        def own_tile(k, carry):
            acc[k, c * n:(c + 1) * n, :] = raw[k, c * n:(c + 1) * n, :] + conv(ext, 0, k, c * n)
            return carry

        lax.fori_loop(0, tiles, own_tile, 0)

    for c in range(blocks):
        extend(ext, lambda k, a, b: raw[k, a:b, :], c)
    pass_block(0)
    own_block(0)

    for d in range(1, groups):
        edge_copy(d).wait_recv()
    steps = min(HALO, groups - 1)
    right = [(groups - 1 - q, lengths[lax.rem(g + 1 + q, groups)]) for q in range(steps)]
    left = [(1 + q, lengths[lax.rem(g + groups - 1 - q, groups)]) for q in range(steps)]
    for j in range(HALO):
        source, slot, passed = right[0][0], jnp.int32(j), jnp.int32(0)
        for q in range(1, steps):
            passed = passed + right[q - 1][1]
            source = jnp.where(passed <= j, right[q][0], source)
            slot = jnp.where(passed <= j, j - passed, slot)
        halo[:, HALO + j:HALO + j + 1, :] = peers[source, :, pl.ds(slot, 1), :]
        back = HALO - j
        source, row, passed = left[0][0], HALO + jnp.minimum(left[0][1], HALO) - back, jnp.int32(0)
        for q in range(1, steps):
            passed = passed + left[q - 1][1]
            reach = passed < back
            source = jnp.where(reach, left[q][0], source)
            row = jnp.where(reach, HALO + jnp.minimum(left[q][1], HALO) - (back - passed), row)
        halo[:, j:j + 1, :] = peers[source, :, pl.ds(jnp.maximum(row, 0), 1), :]

    crossing(lambda side: halo_copy(side).start())
    to_mate(lambda side: halo_copy(side).start())
    for c in range(max(1, blocks - 1), blocks):
        send_block(c)
    for c in range(1, blocks):
        pass_block(c)
        own_block(c)

    crossed(lambda side: halo_copy(side).wait_recv())
    from_mate(lambda side: halo_copy(side).wait_recv())
    around = jnp.zeros((2 * HALO, LANES), jnp.float32)
    for k in range(tiles):
        near = jnp.where(use_above, nb_halo[1, k], nb_halo[0, k])
        from_left, from_right = None, None
        for which, values in ((0, halo[k]), (1, near)):
            lefts = jnp.concatenate([values[0:HALO], around], axis=0)
            rights = jnp.concatenate([around, values[HALO:2 * HALO]], axis=0)
            for tap in range(taps):
                factor = coef[which, k, tap:tap + 1, :]
                if tap < HALO:
                    term = lefts[tap:tap + HALO] * factor
                    from_left = term if from_left is None else from_left + term
                if tap > HALO:
                    term = rights[tap:tap + HALO] * factor
                    from_right = term if from_right is None else from_right + term
        acc[k, 0:HALO, :] += from_left
        tail[k, cap - HALO:cap, :] = from_right
    for copy in weights:
        copy.wait()

    writes = []
    for c in range(blocks):
        from_mate(lambda side: row_copy(side, c, 0).wait_recv())
        crossed(lambda side: row_copy(side, c, 0).wait_recv())
        crossed(lambda side: row_copy(side, c, 1).wait_recv())
        extend(ext_nb, lambda k, a, b: jnp.where(use_above, nb[1, k, a:b, :], nb[0, k, a:b, :]), c)

        def nb_tile(k, squares):
            state = acc[k, c * n:(c + 1) * n, :] + conv(ext_nb, 1, k, c * n) + tail[k, pl.ds(cap + c * n - length, n), :]
            st[k] = state
            return squares + state * state

        squares = lax.fori_loop(0, tiles, nb_tile, jnp.zeros((n, LANES), jnp.float32))
        scale = lax.rsqrt(jnp.sum(squares, axis=1, keepdims=True) * (1.0 / channels) + 1e-05)
        state = jnp.concatenate([st[k] for k in range(tiles)], axis=1)
        normed = (state * scale * gain[...]).astype(jnp.bfloat16)
        total = state + b_out[...]
        for h in range(0, hidden, hid_block):
            pre = jnp.dot(normed, w_in[:, h:h + hid_block], preferred_element_type=jnp.float32) + b_in[:, h:h + hid_block]
            active = (0.5 * pre * (1.0 + lax.erf(pre * SQRT_HALF))).astype(jnp.bfloat16)
            total = total + jnp.dot(active, w_out[h:h + hid_block, :], preferred_element_type=jnp.float32)
        inside = c * n + lax.broadcasted_iota(jnp.int32, total.shape, 0) < length
        out_buf[c * n:(c + 1) * n, :] = jnp.where(inside, -total, -0.0)
        write = pltpu.make_async_copy(
            out_buf.at[pl.ds(c * n, n), :], out_hbm.at[0, pl.ds(c * n, n), :], out_sem.at[c]
        )
        write.start()
        writes.append(write)

    for d in range(1, groups):
        edge_copy(d).wait_send()
    crossing(lambda side: halo_copy(side).wait_send())
    to_mate(lambda side: halo_copy(side).wait_send())
    for c in range(blocks):
        crossing(lambda side: row_copy(side, c, 0).wait_send())
        to_mate(lambda side: row_copy(side, c, 0).wait_send())
        to_mate(lambda side: row_copy(side, c, 1).wait_send())
        passing(lambda side: pass_copy(side, c).wait_send())
    for write in writes:
        write.wait()


def on_device(groups, lat_count, field, piece_lengths, offsets, basis, depth_weight, gain, w_in, b_in, w_out, b_out):
    rows_dev, slot_cap, channels = field.shape
    assert rows_dev == 1 and lat_count % 2 == 0 and basis.shape[2] == 2 and basis.shape[3] == 2 * HALO + 1
    cap = round_up(slot_cap, 8)
    if cap != slot_cap:
        field = jnp.pad(field, ((0, 0), (0, cap - slot_cap), (0, 0)))
    tiles = channels // LANES
    hidden = w_in.shape[1]
    n = block_rows(cap, 120)
    blocks = cap // n
    hid_block = 256 if hidden % 256 == 0 else LANES
    taps = basis.shape[3]
    k_rows = round_up(basis.shape[0], 8)
    hbm = pl.BlockSpec(memory_space=pltpu.HBM)
    f32 = jnp.float32
    out = pl.pallas_call(
        functools.partial(kernel, groups, lat_count, n, hid_block),
        out_shape=jax.ShapeDtypeStruct((1, cap, channels), f32),
        in_specs=[hbm] * 10,
        out_specs=pl.BlockSpec(memory_space=pl.ANY),
        scratch_shapes=[
            pltpu.SMEM(piece_lengths.shape, jnp.int32),
            pltpu.SMEM(offsets.shape, jnp.int32),
            pltpu.VMEM(basis.shape, f32),
            pltpu.VMEM(depth_weight.shape, f32),
            pltpu.VMEM((1, channels), f32),
            pltpu.VMEM((1, hidden), f32),
            pltpu.VMEM((1, channels), f32),
            pltpu.VMEM((tiles, cap, LANES), f32),
            pltpu.VMEM((tiles, 2 * HALO, LANES), f32),
            pltpu.VMEM((groups, tiles, 2 * HALO, LANES), f32),
            pltpu.VMEM((tiles, 2 * HALO, LANES), f32),
            pltpu.VMEM((2, tiles, cap, LANES), f32),
            pltpu.VMEM((2, tiles, 2 * HALO, LANES), f32),
            pltpu.VMEM((tiles, cap + 2 * HALO, LANES), f32),
            pltpu.VMEM((tiles, cap + 2 * HALO, LANES), f32),
            pltpu.VMEM((tiles, 2 * cap + 2 * HALO, LANES), f32),
            pltpu.VMEM((2, k_rows, round_up(taps, 8)), f32),
            pltpu.VMEM((2, tiles, round_up(taps, 8), LANES), f32),
            pltpu.VMEM((tiles, cap, LANES), f32),
            pltpu.VMEM((tiles, n, LANES), f32),
            pltpu.VMEM((cap, channels), f32),
            pltpu.VMEM(w_in.shape, w_in.dtype),
            pltpu.VMEM(w_out.shape, w_out.dtype),
            pltpu.SemaphoreType.DMA((tiles,)),
            pltpu.SemaphoreType.DMA((7,)),
            pltpu.SemaphoreType.DMA((2,)),
            pltpu.SemaphoreType.DMA((groups,)),
            pltpu.SemaphoreType.DMA((groups,)),
            pltpu.SemaphoreType.DMA((2,)),
            pltpu.SemaphoreType.DMA((2,)),
            pltpu.SemaphoreType.DMA((2, blocks, 2)),
            pltpu.SemaphoreType.DMA((2, blocks, 2)),
            pltpu.SemaphoreType.DMA((blocks,)),
            pltpu.SemaphoreType.DMA((blocks,)),
        ],
        compiler_params=pltpu.CompilerParams(
            collective_id=0, has_side_effects=True, vmem_limit_bytes=63 * 1024 * 1024
        ),
        cost_estimate=pl.CostEstimate(flops=4 * cap * channels * hidden, bytes_accessed=6 * 1024 * 1024, transcendentals=0),
    )(
        piece_lengths, offsets, field, basis, depth_weight, gain, w_in, b_in, w_out, b_out,
    )
    return -out[:, :slot_cap, :]


def solution(mesh):
    placed = (P(("ens", "lat"), "lon", None), P(), P(), P(), P(), P(), P(), P(), P(), P())
    return jax.shard_map(
        functools.partial(on_device, mesh.shape["lon"], mesh.shape["lat"]),
        mesh=mesh,
        in_specs=placed,
        out_specs=P(("ens", "lat"), "lon", None),
        check_vma=False,
    )
```

```python
import functools
import jax
import jax.numpy as jnp
from jax import lax
from jax.experimental import pallas as pl
from jax.experimental.pallas import tpu as pltpu
from jax.sharding import PartitionSpec as P

LANES = 128
HALO = 8
MESH = pl.DeviceIdType.MESH
SQRT_HALF = 0.7071067811865476


def round_up(value, step):
    return -(-value // step) * step


def block_rows(total, most):
    return max(rows for rows in range(8, most + 1, 8) if total % rows == 0)


def kernel(
    groups, lat_count, bounds, hid_block,
    lengths_hbm, offsets_hbm, field, basis_hbm, depth_hbm, gain_hbm, w_in_hbm, b_in_hbm, w_out_hbm, b_out_hbm,
    out_hbm,
    lengths, offsets, basis, depth_weight, gain, b_in, b_out,
    raw, edge, peers, halo, nb, nb_halo, ext, ext_nb, tail, terms, coef, acc, st, out_buf, w_in, w_out,
    load_sem, small_sem, weight_sem, edge_send, edge_recv, halo_send, halo_recv, row_send, row_recv, pass_send, out_sem,
):
    cap = raw.shape[1]
    tiles = raw.shape[0]
    channels = tiles * LANES
    taps = basis.shape[3]
    count_k = basis.shape[0]
    blocks = len(bounds) - 1
    hidden = w_in.shape[1]
    g = lax.axis_index("lon")
    t = lax.axis_index("lat")
    above, below = t < lat_count - 1, t > 0

    loads = [
        pltpu.make_async_copy(field.at[0, :, pl.ds(k * LANES, LANES)], raw.at[k], load_sem.at[k])
        for k in range(tiles)
    ]
    weights = [
        pltpu.make_async_copy(w_in_hbm, w_in, weight_sem.at[0]),
        pltpu.make_async_copy(w_out_hbm, w_out, weight_sem.at[1]),
    ]
    pairs = [
        (lengths_hbm, lengths), (offsets_hbm, offsets), (basis_hbm, basis), (depth_hbm, depth_weight),
        (gain_hbm, gain.at[0]), (b_in_hbm, b_in.at[0]), (b_out_hbm, b_out.at[0]),
    ]
    smalls = [pltpu.make_async_copy(source, target, small_sem.at[i]) for i, (source, target) in enumerate(pairs)]
    for copy in loads + smalls + weights:
        copy.start()

    barrier = pltpu.get_barrier_semaphore()

    @pl.when(above)
    def _():
        pl.semaphore_signal(barrier, inc=1, device_id={"lat": t + 1}, device_id_type=MESH)

    @pl.when(below)
    def _():
        pl.semaphore_signal(barrier, inc=1, device_id={"lat": t - 1}, device_id_type=MESH)

    @pl.when(t + 2 < lat_count)
    def _():
        pl.semaphore_signal(barrier, inc=1, device_id={"lat": t + 2}, device_id_type=MESH)

    @pl.when(t >= 2)
    def _():
        pl.semaphore_signal(barrier, inc=1, device_id={"lat": t - 2}, device_id_type=MESH)

    for d in range(1, groups):
        pl.semaphore_signal(barrier, inc=1, device_id={"lon": lax.rem(g + d, groups)}, device_id_type=MESH)

    tail[...] = jnp.zeros_like(tail)
    for target in (ext, ext_nb):
        target[:, 0:HALO, :] = jnp.zeros((tiles, HALO, LANES), jnp.float32)
        target[:, cap + HALO:cap + 2 * HALO, :] = jnp.zeros((tiles, HALO, LANES), jnp.float32)

    smalls[0].wait()
    length = lengths[g]
    for copy in loads:
        copy.wait()
    edge[:, 0:HALO, :] = raw[:, 0:HALO, :]
    for k in range(tiles):
        edge[k, HALO:2 * HALO, :] = raw[k, pl.ds(jnp.maximum(length - HALO, 0), HALO), :]

    greeted = [above, below, t + 2 < lat_count, t >= 2]
    pl.semaphore_wait(barrier, groups - 1 + sum(near.astype(jnp.int32) for near in greeted))

    def edge_copy(d):
        return pltpu.make_async_remote_copy(
            src_ref=edge, dst_ref=peers.at[d], send_sem=edge_send.at[d], recv_sem=edge_recv.at[d],
            device_id={"lon": lax.rem(g + d, groups)}, device_id_type=MESH,
        )

    def span(c):
        first = 0 if c == 0 else bounds[c] + HALO
        last = cap if c == blocks - 1 else bounds[c + 1] + HALO
        return first, last

    def half(c, h):
        first, last = span(c)
        middle = first + round_up((last - first) // 2, 8)
        return pl.ds(first, middle - first) if h == 0 else pl.ds(middle, last - middle)

    def row_copy(side, c, h):
        return pltpu.make_async_remote_copy(
            src_ref=raw.at[:, half(c, h), :], dst_ref=nb.at[side, :, half(c, h), :],
            send_sem=row_send.at[side, c, h], recv_sem=row_recv.at[side, c, h],
            device_id={"lat": t + 1 - 2 * side}, device_id_type=MESH,
        )

    def pass_copy(side, c):
        return pltpu.make_async_remote_copy(
            src_ref=nb.at[1 - side, :, half(c, 1), :], dst_ref=nb.at[side, :, half(c, 1), :],
            send_sem=pass_send.at[c], recv_sem=row_recv.at[side, c, 1],
            device_id={"lat": t + 2 - 4 * side}, device_id_type=MESH,
        )

    def halo_copy(side):
        return pltpu.make_async_remote_copy(
            src_ref=halo, dst_ref=nb_halo.at[side], send_sem=halo_send.at[side], recv_sem=halo_recv.at[side],
            device_id={"lat": t + 1 - 2 * side}, device_id_type=MESH,
        )

    odd = lax.rem(t, 2) == 1

    def crossing(act):
        pl.when(above & odd)(functools.partial(act, 0))
        pl.when(below & ~odd)(functools.partial(act, 1))

    def crossed(act):
        pl.when(above & odd)(functools.partial(act, 1))
        pl.when(below & ~odd)(functools.partial(act, 0))

    def to_mate(act):
        pl.when(~odd)(functools.partial(act, 0))
        pl.when(odd)(functools.partial(act, 1))

    def from_mate(act):
        pl.when(~odd)(functools.partial(act, 1))
        pl.when(odd)(functools.partial(act, 0))

    def passing(act):
        pl.when(~odd & (t + 2 < lat_count))(functools.partial(act, 0))
        pl.when(odd & (t >= 2))(functools.partial(act, 1))

    def send_block(c):
        crossing(lambda side: row_copy(side, c, 0).start())
        to_mate(lambda side: row_copy(side, c, 1).start())
        to_mate(lambda side: row_copy(side, c, 0).start())

    def pass_block(c):
        from_mate(lambda side: row_copy(side, c, 1).wait_recv())
        passing(lambda side: pass_copy(side, c).start())

    send_block(0)
    for d in range(1, groups):
        edge_copy(d).start()
    pass_block(0)

    for d in range(1, groups):
        edge_copy(d).wait_recv()
    steps = min(HALO, groups - 1)
    right = [(groups - 1 - q, lengths[lax.rem(g + 1 + q, groups)]) for q in range(steps)]
    left = [(1 + q, lengths[lax.rem(g + groups - 1 - q, groups)]) for q in range(steps)]
    for j in range(HALO):
        source, slot, passed = right[0][0], jnp.int32(j), jnp.int32(0)
        for q in range(1, steps):
            passed = passed + right[q - 1][1]
            source = jnp.where(passed <= j, right[q][0], source)
            slot = jnp.where(passed <= j, j - passed, slot)
        halo[:, HALO + j:HALO + j + 1, :] = peers[source, :, pl.ds(slot, 1), :]
        back = HALO - j
        source, row, passed = left[0][0], HALO + jnp.minimum(left[0][1], HALO) - back, jnp.int32(0)
        for q in range(1, steps):
            passed = passed + left[q - 1][1]
            reach = passed < back
            source = jnp.where(reach, left[q][0], source)
            row = jnp.where(reach, HALO + jnp.minimum(left[q][1], HALO) - (back - passed), row)
        halo[:, j:j + 1, :] = peers[source, :, pl.ds(jnp.maximum(row, 0), 1), :]

    crossing(lambda side: halo_copy(side).start())
    to_mate(lambda side: halo_copy(side).start())
    for c in range(1, blocks):
        send_block(c)
    for copy in smalls[1:]:
        copy.wait()
    use_above = offsets[t] == t
    terms[...] = jnp.zeros_like(terms)
    for s in range(2):
        for k in range(count_k):
            terms[s, k:k + 1, 0:taps] = basis[k, t, s:s + 1, :]
    weight = jnp.concatenate([depth_weight[...], jnp.zeros((terms.shape[1] - count_k, channels), jnp.float32)], 0)
    both = [
        lax.dot_general(
            terms[s], weight, (((0,), (0,)), ((), ())),
            precision=lax.Precision.HIGHEST, preferred_element_type=jnp.float32,
        )
        for s in range(2)
    ]
    own_coef = jnp.where(use_above, both[0], both[1])
    nb_coef = jnp.where(use_above, both[1], both[0])
    for k in range(tiles):
        coef[0, k] = own_coef[:, k * LANES:(k + 1) * LANES]
        coef[1, k] = nb_coef[:, k * LANES:(k + 1) * LANES]

    def conv(source, which, k, start, n):
        total = None
        for shift in range(HALO):
            reach = n + HALO * ((taps - 1 - shift) // HALO)
            moved = source[k, start + shift:start + shift + reach, :]
            for tap in range(shift, taps, HALO):
                term = moved[tap - shift:tap - shift + n] * coef[which, k, tap:tap + 1, :]
                total = term if total is None else total + term
        return total

    def extend(target, values, c):
        first, last = span(c)

        def tile(k, carry):
            inside = first + lax.broadcasted_iota(jnp.int32, (last - first, LANES), 0) < length
            target[k, HALO + first:HALO + last, :] = jnp.where(inside, values(k, first, last), 0.0)
            return carry

        lax.fori_loop(0, tiles, tile, 0)

    def own_block(c):
        start, n = bounds[c], bounds[c + 1] - bounds[c]

        def own_tile(k, carry):
            acc[k, start:start + n, :] = raw[k, start:start + n, :] + conv(ext, 0, k, start, n)
            return carry

        lax.fori_loop(0, tiles, own_tile, 0)

    for c in range(blocks):
        extend(ext, lambda k, a, b: raw[k, a:b, :], c)

    for c in range(blocks):
        if c + 1 < blocks:
            pass_block(c + 1)
        own_block(c)

    crossed(lambda side: halo_copy(side).wait_recv())
    from_mate(lambda side: halo_copy(side).wait_recv())
    around = jnp.zeros((2 * HALO, LANES), jnp.float32)
    for k in range(tiles):
        near = jnp.where(use_above, nb_halo[1, k], nb_halo[0, k])
        from_left, from_right = None, None
        for which, values in ((0, halo[k]), (1, near)):
            lefts = jnp.concatenate([values[0:HALO], around], axis=0)
            rights = jnp.concatenate([around, values[HALO:2 * HALO]], axis=0)
            for tap in range(taps):
                factor = coef[which, k, tap:tap + 1, :]
                if tap < HALO:
                    term = lefts[tap:tap + HALO] * factor
                    from_left = term if from_left is None else from_left + term
                if tap > HALO:
                    term = rights[tap:tap + HALO] * factor
                    from_right = term if from_right is None else from_right + term
        acc[k, 0:HALO, :] += from_left
        tail[k, cap - HALO:cap, :] = from_right
    for copy in weights:
        copy.wait()

    writes = []
    for c in range(blocks):
        from_mate(lambda side: row_copy(side, c, 0).wait_recv())
        crossed(lambda side: row_copy(side, c, 0).wait_recv())
        crossed(lambda side: row_copy(side, c, 1).wait_recv())
        extend(ext_nb, lambda k, a, b: jnp.where(use_above, nb[1, k, a:b, :], nb[0, k, a:b, :]), c)

        start, n = bounds[c], bounds[c + 1] - bounds[c]

        def nb_tile(k, squares):
            state = acc[k, start:start + n, :] + conv(ext_nb, 1, k, start, n) + tail[k, pl.ds(cap + start - length, n), :]
            st[k, 0:n, :] = state
            return squares + state * state

        squares = lax.fori_loop(0, tiles, nb_tile, jnp.zeros((n, LANES), jnp.float32))
        scale = lax.rsqrt(jnp.sum(squares, axis=1, keepdims=True) * (1.0 / channels) + 1e-05)
        state = jnp.concatenate([st[k, 0:n, :] for k in range(tiles)], axis=1)
        normed = (state * scale * gain[...]).astype(jnp.bfloat16)
        total = state + b_out[...]
        for h in range(0, hidden, hid_block):
            pre = jnp.dot(normed, w_in[:, h:h + hid_block], preferred_element_type=jnp.float32) + b_in[:, h:h + hid_block]
            active = (0.5 * pre * (1.0 + lax.erf(pre * SQRT_HALF))).astype(jnp.bfloat16)
            total = total + jnp.dot(active, w_out[h:h + hid_block, :], preferred_element_type=jnp.float32)
        inside = start + lax.broadcasted_iota(jnp.int32, total.shape, 0) < length
        out_buf[start:start + n, :] = jnp.where(inside, total, 0.0)
        write = pltpu.make_async_copy(
            out_buf.at[pl.ds(start, n), :], out_hbm.at[0, pl.ds(start, n), :], out_sem.at[c]
        )
        write.start()
        writes.append(write)

    for d in range(1, groups):
        edge_copy(d).wait_send()
    crossing(lambda side: halo_copy(side).wait_send())
    to_mate(lambda side: halo_copy(side).wait_send())
    for c in range(blocks):
        crossing(lambda side: row_copy(side, c, 0).wait_send())
        to_mate(lambda side: row_copy(side, c, 0).wait_send())
        to_mate(lambda side: row_copy(side, c, 1).wait_send())
        passing(lambda side: pass_copy(side, c).wait_send())
    for write in writes:
        write.wait()


def hand_over(rows, source, target, held, in_sem, out_sem):
    pieces = [pl.ds(first, rows) for first in range(0, held.shape[0], rows)]
    takes = [pltpu.make_async_copy(source.at[0, piece, :], held.at[piece, :], in_sem.at[i]) for i, piece in enumerate(pieces)]
    gives = [pltpu.make_async_copy(held.at[piece, :], target.at[0, piece, :], out_sem.at[i]) for i, piece in enumerate(pieces)]
    for take in takes:
        take.start()
    for take, give in zip(takes, gives):
        take.wait()
        give.start()
    for give in gives:
        give.wait()


def on_device(groups, lat_count, field, piece_lengths, offsets, basis, depth_weight, gain, w_in, b_in, w_out, b_out):
    rows_dev, slot_cap, channels = field.shape
    assert rows_dev == 1 and lat_count % 2 == 0 and basis.shape[2] == 2 and basis.shape[3] == 2 * HALO + 1
    cap = round_up(slot_cap, 8)
    if cap != slot_cap:
        field = jnp.pad(field, ((0, 0), (0, cap - slot_cap), (0, 0)))
    tiles = channels // LANES
    hidden = w_in.shape[1]
    third, fifth = cap // 3, cap // 5
    bounds = (0, third, 2 * third, 2 * third + fifth, cap) if cap % 120 == 0 else (0, cap)
    blocks = len(bounds) - 1
    n = max(bounds[c + 1] - bounds[c] for c in range(blocks))
    hid_block = 256 if hidden % 256 == 0 else LANES
    taps = basis.shape[3]
    k_rows = round_up(basis.shape[0], 8)
    hbm = pl.BlockSpec(memory_space=pltpu.HBM)
    f32 = jnp.float32
    out = pl.pallas_call(
        functools.partial(kernel, groups, lat_count, bounds, hid_block),
        out_shape=jax.ShapeDtypeStruct((1, cap, channels), f32),
        in_specs=[hbm] * 10,
        out_specs=pl.BlockSpec(memory_space=pl.ANY),
        scratch_shapes=[
            pltpu.SMEM(piece_lengths.shape, jnp.int32),
            pltpu.SMEM(offsets.shape, jnp.int32),
            pltpu.VMEM(basis.shape, f32),
            pltpu.VMEM(depth_weight.shape, f32),
            pltpu.VMEM((1, channels), f32),
            pltpu.VMEM((1, hidden), f32),
            pltpu.VMEM((1, channels), f32),
            pltpu.VMEM((tiles, cap, LANES), f32),
            pltpu.VMEM((tiles, 2 * HALO, LANES), f32),
            pltpu.VMEM((groups, tiles, 2 * HALO, LANES), f32),
            pltpu.VMEM((tiles, 2 * HALO, LANES), f32),
            pltpu.VMEM((2, tiles, cap, LANES), f32),
            pltpu.VMEM((2, tiles, 2 * HALO, LANES), f32),
            pltpu.VMEM((tiles, cap + 2 * HALO, LANES), f32),
            pltpu.VMEM((tiles, cap + 2 * HALO, LANES), f32),
            pltpu.VMEM((tiles, 2 * cap + 2 * HALO, LANES), f32),
            pltpu.VMEM((2, k_rows, round_up(taps, 8)), f32),
            pltpu.VMEM((2, tiles, round_up(taps, 8), LANES), f32),
            pltpu.VMEM((tiles, cap, LANES), f32),
            pltpu.VMEM((tiles, n, LANES), f32),
            pltpu.VMEM((cap, channels), f32),
            pltpu.VMEM(w_in.shape, w_in.dtype),
            pltpu.VMEM(w_out.shape, w_out.dtype),
            pltpu.SemaphoreType.DMA((tiles,)),
            pltpu.SemaphoreType.DMA((7,)),
            pltpu.SemaphoreType.DMA((2,)),
            pltpu.SemaphoreType.DMA((groups,)),
            pltpu.SemaphoreType.DMA((groups,)),
            pltpu.SemaphoreType.DMA((2,)),
            pltpu.SemaphoreType.DMA((2,)),
            pltpu.SemaphoreType.DMA((2, blocks, 2)),
            pltpu.SemaphoreType.DMA((2, blocks, 2)),
            pltpu.SemaphoreType.DMA((blocks,)),
            pltpu.SemaphoreType.DMA((blocks,)),
        ],
        compiler_params=pltpu.CompilerParams(
            collective_id=0, has_side_effects=True, vmem_limit_bytes=63 * 1024 * 1024
        ),
        cost_estimate=pl.CostEstimate(flops=4 * cap * channels * hidden, bytes_accessed=6 * 1024 * 1024, transcendentals=0),
    )(
        piece_lengths, offsets, field, basis, depth_weight, gain, w_in, b_in, w_out, b_out,
    )
    rows = block_rows(cap, 72)
    out = pl.pallas_call(
        functools.partial(hand_over, rows),
        out_shape=jax.ShapeDtypeStruct(out.shape, f32),
        in_specs=[hbm],
        out_specs=hbm,
        scratch_shapes=[
            pltpu.VMEM((cap, channels), f32),
            pltpu.SemaphoreType.DMA((cap // rows,)),
            pltpu.SemaphoreType.DMA((cap // rows,)),
        ],
        compiler_params=pltpu.CompilerParams(vmem_limit_bytes=63 * 1024 * 1024),
    )(out)
    return out[:, :slot_cap, :]


def solution(mesh):
    placed = (P(("ens", "lat"), "lon", None), P(), P(), P(), P(), P(), P(), P(), P(), P())
    return jax.shard_map(
        functools.partial(on_device, mesh.shape["lon"], mesh.shape["lat"]),
        mesh=mesh,
        in_specs=placed,
        out_specs=P(("ens", "lat"), "lon", None),
        check_vma=False,
    )
```

```python
import functools
import jax
import jax.numpy as jnp
from jax import lax
from jax.experimental import pallas as pl
from jax.experimental.pallas import tpu as pltpu
from jax.sharding import PartitionSpec as P

LANES = 128
HALO = 8
MESH = pl.DeviceIdType.MESH
SQRT_HALF = 0.7071067811865476


def round_up(value, step):
    return -(-value // step) * step


def block_rows(total, most):
    return max(rows for rows in range(8, most + 1, 8) if total % rows == 0)


def kernel(
    groups, lat_count, bounds, hid_block,
    lengths_hbm, offsets_hbm, field, basis_hbm, depth_hbm, gain_hbm, w_in_hbm, b_in_hbm, w_out_hbm, b_out_hbm,
    out_hbm,
    lengths, offsets, basis, depth_weight, gain, b_in, b_out,
    raw, edge, peers, halo, nb, nb_halo, ext, ext_nb, tail, terms, coef, acc, st, out_buf, w_in, w_out,
    load_sem, small_sem, weight_sem, edge_send, edge_recv, halo_send, halo_recv, row_send, row_recv, pass_send, out_sem,
):
    cap = raw.shape[1]
    tiles = raw.shape[0]
    channels = tiles * LANES
    taps = basis.shape[3]
    count_k = basis.shape[0]
    blocks = len(bounds) - 1
    hidden = w_in.shape[1]
    g = lax.axis_index("lon")
    t = lax.axis_index("lat")
    above, below = t < lat_count - 1, t > 0

    loads = [
        pltpu.make_async_copy(field.at[0, :, pl.ds(k * LANES, LANES)], raw.at[k], load_sem.at[k])
        for k in range(tiles)
    ]
    weights = [
        pltpu.make_async_copy(w_in_hbm, w_in, weight_sem.at[0]),
        pltpu.make_async_copy(w_out_hbm, w_out, weight_sem.at[1]),
    ]
    pairs = [
        (lengths_hbm, lengths), (offsets_hbm, offsets), (basis_hbm, basis), (depth_hbm, depth_weight),
        (gain_hbm, gain.at[0]), (b_in_hbm, b_in.at[0]), (b_out_hbm, b_out.at[0]),
    ]
    smalls = [pltpu.make_async_copy(source, target, small_sem.at[i]) for i, (source, target) in enumerate(pairs)]
    for copy in loads + smalls + weights:
        copy.start()

    barrier = pltpu.get_barrier_semaphore()

    @pl.when(above)
    def _():
        pl.semaphore_signal(barrier, inc=1, device_id={"lat": t + 1}, device_id_type=MESH)

    @pl.when(below)
    def _():
        pl.semaphore_signal(barrier, inc=1, device_id={"lat": t - 1}, device_id_type=MESH)

    @pl.when(t + 2 < lat_count)
    def _():
        pl.semaphore_signal(barrier, inc=1, device_id={"lat": t + 2}, device_id_type=MESH)

    @pl.when(t >= 2)
    def _():
        pl.semaphore_signal(barrier, inc=1, device_id={"lat": t - 2}, device_id_type=MESH)

    for d in range(1, groups):
        pl.semaphore_signal(barrier, inc=1, device_id={"lon": lax.rem(g + d, groups)}, device_id_type=MESH)

    tail[...] = jnp.zeros_like(tail)
    for target in (ext, ext_nb):
        target[:, 0:HALO, :] = jnp.zeros((tiles, HALO, LANES), jnp.float32)
        target[:, cap + HALO:cap + 2 * HALO, :] = jnp.zeros((tiles, HALO, LANES), jnp.float32)

    smalls[0].wait()
    length = lengths[g]
    for copy in loads:
        copy.wait()
    edge[:, 0:HALO, :] = raw[:, 0:HALO, :]
    for k in range(tiles):
        edge[k, HALO:2 * HALO, :] = raw[k, pl.ds(jnp.maximum(length - HALO, 0), HALO), :]

    greeted = [above, below, t + 2 < lat_count, t >= 2]
    pl.semaphore_wait(barrier, groups - 1 + sum(near.astype(jnp.int32) for near in greeted))

    def edge_copy(d):
        return pltpu.make_async_remote_copy(
            src_ref=edge, dst_ref=peers.at[d], send_sem=edge_send.at[d], recv_sem=edge_recv.at[d],
            device_id={"lon": lax.rem(g + d, groups)}, device_id_type=MESH,
        )

    def span(c):
        first = 0 if c == 0 else bounds[c] + HALO
        last = cap if c == blocks - 1 else bounds[c + 1] + HALO
        return first, last

    def half(c, h):
        first, last = span(c)
        middle = first + round_up((last - first) // 2, 8)
        return pl.ds(first, middle - first) if h == 0 else pl.ds(middle, last - middle)

    def row_copy(side, c, h):
        return pltpu.make_async_remote_copy(
            src_ref=raw.at[:, half(c, h), :], dst_ref=nb.at[side, :, half(c, h), :],
            send_sem=row_send.at[side, c, h], recv_sem=row_recv.at[side, c, h],
            device_id={"lat": t + 1 - 2 * side}, device_id_type=MESH,
        )

    def pass_copy(side, c):
        return pltpu.make_async_remote_copy(
            src_ref=nb.at[1 - side, :, half(c, 1), :], dst_ref=nb.at[side, :, half(c, 1), :],
            send_sem=pass_send.at[c], recv_sem=row_recv.at[side, c, 1],
            device_id={"lat": t + 2 - 4 * side}, device_id_type=MESH,
        )

    def halo_copy(side):
        return pltpu.make_async_remote_copy(
            src_ref=halo, dst_ref=nb_halo.at[side], send_sem=halo_send.at[side], recv_sem=halo_recv.at[side],
            device_id={"lat": t + 1 - 2 * side}, device_id_type=MESH,
        )

    odd = lax.rem(t, 2) == 1

    def crossing(act):
        pl.when(above & odd)(functools.partial(act, 0))
        pl.when(below & ~odd)(functools.partial(act, 1))

    def crossed(act):
        pl.when(above & odd)(functools.partial(act, 1))
        pl.when(below & ~odd)(functools.partial(act, 0))

    def to_mate(act):
        pl.when(~odd)(functools.partial(act, 0))
        pl.when(odd)(functools.partial(act, 1))

    def from_mate(act):
        pl.when(~odd)(functools.partial(act, 1))
        pl.when(odd)(functools.partial(act, 0))

    def passing(act):
        pl.when(~odd & (t + 2 < lat_count))(functools.partial(act, 0))
        pl.when(odd & (t >= 2))(functools.partial(act, 1))

    def cross_block(c):
        crossing(lambda side: row_copy(side, c, 0).start())

    def mate_block(c):
        to_mate(lambda side: row_copy(side, c, 1).start())
        to_mate(lambda side: row_copy(side, c, 0).start())

    def pass_block(c):
        from_mate(lambda side: row_copy(side, c, 1).wait_recv())
        passing(lambda side: pass_copy(side, c).start())

    cross_block(0)
    mate_block(0)
    for d in range(1, groups):
        edge_copy(d).start()
    pass_block(0)

    for d in range(1, groups):
        edge_copy(d).wait_recv()
    steps = min(HALO, groups - 1)
    right = [(groups - 1 - q, lengths[lax.rem(g + 1 + q, groups)]) for q in range(steps)]
    left = [(1 + q, lengths[lax.rem(g + groups - 1 - q, groups)]) for q in range(steps)]
    for j in range(HALO):
        source, slot, passed = right[0][0], jnp.int32(j), jnp.int32(0)
        for q in range(1, steps):
            passed = passed + right[q - 1][1]
            source = jnp.where(passed <= j, right[q][0], source)
            slot = jnp.where(passed <= j, j - passed, slot)
        halo[:, HALO + j:HALO + j + 1, :] = peers[source, :, pl.ds(slot, 1), :]
        back = HALO - j
        source, row, passed = left[0][0], HALO + jnp.minimum(left[0][1], HALO) - back, jnp.int32(0)
        for q in range(1, steps):
            passed = passed + left[q - 1][1]
            reach = passed < back
            source = jnp.where(reach, left[q][0], source)
            row = jnp.where(reach, HALO + jnp.minimum(left[q][1], HALO) - (back - passed), row)
        halo[:, j:j + 1, :] = peers[source, :, pl.ds(jnp.maximum(row, 0), 1), :]

    crossing(lambda side: halo_copy(side).start())
    to_mate(lambda side: halo_copy(side).start())
    for c in range(1, blocks):
        if c == 1:
            cross_block(c)
        mate_block(c)
    for copy in smalls[1:]:
        copy.wait()
    use_above = offsets[t] == t
    terms[...] = jnp.zeros_like(terms)
    for s in range(2):
        for k in range(count_k):
            terms[s, k:k + 1, 0:taps] = basis[k, t, s:s + 1, :]
    weight = jnp.concatenate([depth_weight[...], jnp.zeros((terms.shape[1] - count_k, channels), jnp.float32)], 0)
    both = [
        lax.dot_general(
            terms[s], weight, (((0,), (0,)), ((), ())),
            precision=lax.Precision.HIGHEST, preferred_element_type=jnp.float32,
        )
        for s in range(2)
    ]
    own_coef = jnp.where(use_above, both[0], both[1])
    nb_coef = jnp.where(use_above, both[1], both[0])
    for k in range(tiles):
        coef[0, k] = own_coef[:, k * LANES:(k + 1) * LANES]
        coef[1, k] = nb_coef[:, k * LANES:(k + 1) * LANES]

    def conv(source, which, k, start, n):
        total = None
        for shift in range(HALO):
            reach = n + HALO * ((taps - 1 - shift) // HALO)
            moved = source[k, start + shift:start + shift + reach, :]
            for tap in range(shift, taps, HALO):
                term = moved[tap - shift:tap - shift + n] * coef[which, k, tap:tap + 1, :]
                total = term if total is None else total + term
        return total

    def extend(target, values, c):
        first, last = span(c)

        def tile(k, carry):
            inside = first + lax.broadcasted_iota(jnp.int32, (last - first, LANES), 0) < length
            target[k, HALO + first:HALO + last, :] = jnp.where(inside, values(k, first, last), 0.0)
            return carry

        lax.fori_loop(0, tiles, tile, 0)

    def own_block(c):
        start, n = bounds[c], bounds[c + 1] - bounds[c]

        def own_tile(k, carry):
            acc[k, start:start + n, :] = raw[k, start:start + n, :] + conv(ext, 0, k, start, n)
            return carry

        lax.fori_loop(0, tiles, own_tile, 0)

    for c in range(blocks):
        extend(ext, lambda k, a, b: raw[k, a:b, :], c)

    for c in range(blocks):
        if c == 0 and blocks > 1:
            pass_block(1)
        if c == blocks - 1 and blocks > 2:
            pass_block(2)
            cross_block(2)
        own_block(c)

    crossed(lambda side: halo_copy(side).wait_recv())
    from_mate(lambda side: halo_copy(side).wait_recv())
    around = jnp.zeros((2 * HALO, LANES), jnp.float32)
    for k in range(tiles):
        near = jnp.where(use_above, nb_halo[1, k], nb_halo[0, k])
        from_left, from_right = None, None
        for which, values in ((0, halo[k]), (1, near)):
            lefts = jnp.concatenate([values[0:HALO], around], axis=0)
            rights = jnp.concatenate([around, values[HALO:2 * HALO]], axis=0)
            for tap in range(taps):
                factor = coef[which, k, tap:tap + 1, :]
                if tap < HALO:
                    term = lefts[tap:tap + HALO] * factor
                    from_left = term if from_left is None else from_left + term
                if tap > HALO:
                    term = rights[tap:tap + HALO] * factor
                    from_right = term if from_right is None else from_right + term
        acc[k, 0:HALO, :] += from_left
        tail[k, cap - HALO:cap, :] = from_right
    for copy in weights:
        copy.wait()

    writes = []
    for c in range(blocks):
        if 0 < c and c + 2 < blocks:
            pass_block(c + 2)
            cross_block(c + 2)
        from_mate(lambda side: row_copy(side, c, 0).wait_recv())
        crossed(lambda side: row_copy(side, c, 0).wait_recv())
        crossed(lambda side: row_copy(side, c, 1).wait_recv())
        extend(ext_nb, lambda k, a, b: jnp.where(use_above, nb[1, k, a:b, :], nb[0, k, a:b, :]), c)

        start, n = bounds[c], bounds[c + 1] - bounds[c]

        def nb_tile(k, squares):
            state = acc[k, start:start + n, :] + conv(ext_nb, 1, k, start, n) + tail[k, pl.ds(cap + start - length, n), :]
            st[k, 0:n, :] = state
            return squares + state * state

        squares = lax.fori_loop(0, tiles, nb_tile, jnp.zeros((n, LANES), jnp.float32))
        scale = lax.rsqrt(jnp.sum(squares, axis=1, keepdims=True) * (1.0 / channels) + 1e-05)
        state = jnp.concatenate([st[k, 0:n, :] for k in range(tiles)], axis=1)
        normed = (state * scale * gain[...]).astype(jnp.bfloat16)
        total = state + b_out[...]
        for h in range(0, hidden, hid_block):
            pre = jnp.dot(normed, w_in[:, h:h + hid_block], preferred_element_type=jnp.float32) + b_in[:, h:h + hid_block]
            active = (0.5 * pre * (1.0 + lax.erf(pre * SQRT_HALF))).astype(jnp.bfloat16)
            total = total + jnp.dot(active, w_out[h:h + hid_block, :], preferred_element_type=jnp.float32)
        inside = start + lax.broadcasted_iota(jnp.int32, total.shape, 0) < length
        out_buf[start:start + n, :] = jnp.where(inside, total, 0.0)
        write = pltpu.make_async_copy(
            out_buf.at[pl.ds(start, n), :], out_hbm.at[0, pl.ds(start, n), :], out_sem.at[c]
        )
        write.start()
        writes.append(write)

    for d in range(1, groups):
        edge_copy(d).wait_send()
    crossing(lambda side: halo_copy(side).wait_send())
    to_mate(lambda side: halo_copy(side).wait_send())
    for c in range(blocks):
        crossing(lambda side: row_copy(side, c, 0).wait_send())
        to_mate(lambda side: row_copy(side, c, 0).wait_send())
        to_mate(lambda side: row_copy(side, c, 1).wait_send())
        passing(lambda side: pass_copy(side, c).wait_send())
    for write in writes:
        write.wait()


def hand_over(rows, source, target, held, in_sem, out_sem):
    pieces = [pl.ds(first, rows) for first in range(0, held.shape[0], rows)]
    takes = [pltpu.make_async_copy(source.at[0, piece, :], held.at[piece, :], in_sem.at[i]) for i, piece in enumerate(pieces)]
    gives = [pltpu.make_async_copy(held.at[piece, :], target.at[0, piece, :], out_sem.at[i]) for i, piece in enumerate(pieces)]
    for take in takes:
        take.start()
    for take, give in zip(takes, gives):
        take.wait()
        give.start()
    for give in gives:
        give.wait()


def on_device(groups, lat_count, field, piece_lengths, offsets, basis, depth_weight, gain, w_in, b_in, w_out, b_out):
    rows_dev, slot_cap, channels = field.shape
    assert rows_dev == 1 and lat_count % 2 == 0 and basis.shape[2] == 2 and basis.shape[3] == 2 * HALO + 1
    cap = round_up(slot_cap, 8)
    if cap != slot_cap:
        field = jnp.pad(field, ((0, 0), (0, cap - slot_cap), (0, 0)))
    tiles = channels // LANES
    hidden = w_in.shape[1]
    third, fifth = cap // 3, cap // 5
    bounds = (0, third, 2 * third, 2 * third + fifth, cap) if cap % 120 == 0 else (0, cap)
    blocks = len(bounds) - 1
    n = max(bounds[c + 1] - bounds[c] for c in range(blocks))
    hid_block = 256 if hidden % 256 == 0 else LANES
    taps = basis.shape[3]
    k_rows = round_up(basis.shape[0], 8)
    hbm = pl.BlockSpec(memory_space=pltpu.HBM)
    f32 = jnp.float32
    out = pl.pallas_call(
        functools.partial(kernel, groups, lat_count, bounds, hid_block),
        out_shape=jax.ShapeDtypeStruct((1, cap, channels), f32),
        in_specs=[hbm] * 10,
        out_specs=pl.BlockSpec(memory_space=pl.ANY),
        scratch_shapes=[
            pltpu.SMEM(piece_lengths.shape, jnp.int32),
            pltpu.SMEM(offsets.shape, jnp.int32),
            pltpu.VMEM(basis.shape, f32),
            pltpu.VMEM(depth_weight.shape, f32),
            pltpu.VMEM((1, channels), f32),
            pltpu.VMEM((1, hidden), f32),
            pltpu.VMEM((1, channels), f32),
            pltpu.VMEM((tiles, cap, LANES), f32),
            pltpu.VMEM((tiles, 2 * HALO, LANES), f32),
            pltpu.VMEM((groups, tiles, 2 * HALO, LANES), f32),
            pltpu.VMEM((tiles, 2 * HALO, LANES), f32),
            pltpu.VMEM((2, tiles, cap, LANES), f32),
            pltpu.VMEM((2, tiles, 2 * HALO, LANES), f32),
            pltpu.VMEM((tiles, cap + 2 * HALO, LANES), f32),
            pltpu.VMEM((tiles, cap + 2 * HALO, LANES), f32),
            pltpu.VMEM((tiles, 2 * cap + 2 * HALO, LANES), f32),
            pltpu.VMEM((2, k_rows, round_up(taps, 8)), f32),
            pltpu.VMEM((2, tiles, round_up(taps, 8), LANES), f32),
            pltpu.VMEM((tiles, cap, LANES), f32),
            pltpu.VMEM((tiles, n, LANES), f32),
            pltpu.VMEM((cap, channels), f32),
            pltpu.VMEM(w_in.shape, w_in.dtype),
            pltpu.VMEM(w_out.shape, w_out.dtype),
            pltpu.SemaphoreType.DMA((tiles,)),
            pltpu.SemaphoreType.DMA((7,)),
            pltpu.SemaphoreType.DMA((2,)),
            pltpu.SemaphoreType.DMA((groups,)),
            pltpu.SemaphoreType.DMA((groups,)),
            pltpu.SemaphoreType.DMA((2,)),
            pltpu.SemaphoreType.DMA((2,)),
            pltpu.SemaphoreType.DMA((2, blocks, 2)),
            pltpu.SemaphoreType.DMA((2, blocks, 2)),
            pltpu.SemaphoreType.DMA((blocks,)),
            pltpu.SemaphoreType.DMA((blocks,)),
        ],
        compiler_params=pltpu.CompilerParams(
            collective_id=0, has_side_effects=True, vmem_limit_bytes=63 * 1024 * 1024
        ),
        cost_estimate=pl.CostEstimate(flops=4 * cap * channels * hidden, bytes_accessed=6 * 1024 * 1024, transcendentals=0),
    )(
        piece_lengths, offsets, field, basis, depth_weight, gain, w_in, b_in, w_out, b_out,
    )
    rows = block_rows(cap, 72)
    out = pl.pallas_call(
        functools.partial(hand_over, rows),
        out_shape=jax.ShapeDtypeStruct(out.shape, f32),
        in_specs=[hbm],
        out_specs=hbm,
        scratch_shapes=[
            pltpu.VMEM((cap, channels), f32),
            pltpu.SemaphoreType.DMA((cap // rows,)),
            pltpu.SemaphoreType.DMA((cap // rows,)),
        ],
        compiler_params=pltpu.CompilerParams(vmem_limit_bytes=63 * 1024 * 1024),
    )(out)
    return out[:, :slot_cap, :]


def solution(mesh):
    placed = (P(("ens", "lat"), "lon", None), P(), P(), P(), P(), P(), P(), P(), P(), P())
    return jax.shard_map(
        functools.partial(on_device, mesh.shape["lon"], mesh.shape["lat"]),
        mesh=mesh,
        in_specs=placed,
        out_specs=P(("ens", "lat"), "lon", None),
        check_vma=False,
    )
```

```python
import functools
import jax
import jax.numpy as jnp
from jax import lax
from jax.experimental import pallas as pl
from jax.experimental.pallas import tpu as pltpu
from jax.sharding import PartitionSpec as P

LANES = 128
HALO = 8
MESH = pl.DeviceIdType.MESH
SQRT_HALF = 0.7071067811865476


def round_up(value, step):
    return -(-value // step) * step


def block_rows(total, most):
    return max(rows for rows in range(8, most + 1, 8) if total % rows == 0)


def kernel(
    groups, lat_count, bounds, hid_block,
    lengths_hbm, offsets_hbm, field, basis_hbm, depth_hbm, gain_hbm, w_in_hbm, b_in_hbm, w_out_hbm, b_out_hbm,
    out_hbm,
    lengths, offsets, basis, depth_weight, gain, b_in, b_out,
    raw, edge, peers, halo, nb, nb_halo, ext, ext_nb, tail, terms, coef, acc, st, out_buf, w_in, w_out,
    load_sem, small_sem, weight_sem, edge_send, edge_recv, halo_send, halo_recv, row_send, row_recv, pass_send, out_sem,
):
    cap = raw.shape[1]
    tiles = raw.shape[0]
    channels = tiles * LANES
    taps = basis.shape[3]
    count_k = basis.shape[0]
    blocks = len(bounds) - 1
    hidden = w_in.shape[1]
    g = lax.axis_index("lon")
    t = lax.axis_index("lat")
    above, below = t < lat_count - 1, t > 0

    loads = [
        pltpu.make_async_copy(field.at[0, :, pl.ds(k * LANES, LANES)], raw.at[k], load_sem.at[k])
        for k in range(tiles)
    ]
    weights = [
        pltpu.make_async_copy(w_in_hbm, w_in, weight_sem.at[0]),
        pltpu.make_async_copy(w_out_hbm, w_out, weight_sem.at[1]),
    ]
    pairs = [
        (lengths_hbm, lengths), (offsets_hbm, offsets), (basis_hbm, basis), (depth_hbm, depth_weight),
        (gain_hbm, gain.at[0]), (b_in_hbm, b_in.at[0]), (b_out_hbm, b_out.at[0]),
    ]
    smalls = [pltpu.make_async_copy(source, target, small_sem.at[i]) for i, (source, target) in enumerate(pairs)]
    for copy in loads + smalls + weights:
        copy.start()

    barrier = pltpu.get_barrier_semaphore()

    @pl.when(above)
    def _():
        pl.semaphore_signal(barrier, inc=1, device_id={"lat": t + 1}, device_id_type=MESH)

    @pl.when(below)
    def _():
        pl.semaphore_signal(barrier, inc=1, device_id={"lat": t - 1}, device_id_type=MESH)

    @pl.when(t + 2 < lat_count)
    def _():
        pl.semaphore_signal(barrier, inc=1, device_id={"lat": t + 2}, device_id_type=MESH)

    @pl.when(t >= 2)
    def _():
        pl.semaphore_signal(barrier, inc=1, device_id={"lat": t - 2}, device_id_type=MESH)

    for d in range(1, groups):
        pl.semaphore_signal(barrier, inc=1, device_id={"lon": lax.rem(g + d, groups)}, device_id_type=MESH)

    tail[...] = jnp.zeros_like(tail)
    for target in (ext, ext_nb):
        target[:, 0:HALO, :] = jnp.zeros((tiles, HALO, LANES), jnp.float32)
        target[:, cap + HALO:cap + 2 * HALO, :] = jnp.zeros((tiles, HALO, LANES), jnp.float32)

    smalls[0].wait()
    length = lengths[g]
    for copy in loads:
        copy.wait()
    edge[:, 0:HALO, :] = raw[:, 0:HALO, :]
    for k in range(tiles):
        edge[k, HALO:2 * HALO, :] = raw[k, pl.ds(jnp.maximum(length - HALO, 0), HALO), :]

    greeted = [above, below, t + 2 < lat_count, t >= 2]
    pl.semaphore_wait(barrier, groups - 1 + sum(near.astype(jnp.int32) for near in greeted))

    def edge_copy(d):
        return pltpu.make_async_remote_copy(
            src_ref=edge, dst_ref=peers.at[d], send_sem=edge_send.at[d], recv_sem=edge_recv.at[d],
            device_id={"lon": lax.rem(g + d, groups)}, device_id_type=MESH,
        )

    def span(c):
        first = 0 if c == 0 else bounds[c] + HALO
        last = cap if c == blocks - 1 else bounds[c + 1] + HALO
        return first, last

    def half(c, h):
        first, last = span(c)
        middle = first + round_up((last - first) // 2, 8)
        return pl.ds(first, middle - first) if h == 0 else pl.ds(middle, last - middle)

    def row_copy(side, c, h):
        return pltpu.make_async_remote_copy(
            src_ref=raw.at[:, half(c, h), :], dst_ref=nb.at[side, :, half(c, h), :],
            send_sem=row_send.at[side, c, h], recv_sem=row_recv.at[side, c, h],
            device_id={"lat": t + 1 - 2 * side}, device_id_type=MESH,
        )

    def pass_copy(side, c):
        return pltpu.make_async_remote_copy(
            src_ref=nb.at[1 - side, :, half(c, 1), :], dst_ref=nb.at[side, :, half(c, 1), :],
            send_sem=pass_send.at[c], recv_sem=row_recv.at[side, c, 1],
            device_id={"lat": t + 2 - 4 * side}, device_id_type=MESH,
        )

    def halo_copy(side):
        return pltpu.make_async_remote_copy(
            src_ref=halo, dst_ref=nb_halo.at[side], send_sem=halo_send.at[side], recv_sem=halo_recv.at[side],
            device_id={"lat": t + 1 - 2 * side}, device_id_type=MESH,
        )

    odd = lax.rem(t, 2) == 1

    def crossing(act):
        pl.when(above & odd)(functools.partial(act, 0))
        pl.when(below & ~odd)(functools.partial(act, 1))

    def crossed(act):
        pl.when(above & odd)(functools.partial(act, 1))
        pl.when(below & ~odd)(functools.partial(act, 0))

    def to_mate(act):
        pl.when(~odd)(functools.partial(act, 0))
        pl.when(odd)(functools.partial(act, 1))

    def from_mate(act):
        pl.when(~odd)(functools.partial(act, 1))
        pl.when(odd)(functools.partial(act, 0))

    def passing(act):
        pl.when(~odd & (t + 2 < lat_count))(functools.partial(act, 0))
        pl.when(odd & (t >= 2))(functools.partial(act, 1))

    def send_block(c):
        crossing(lambda side: row_copy(side, c, 0).start())
        to_mate(lambda side: row_copy(side, c, 1).start())
        to_mate(lambda side: row_copy(side, c, 0).start())

    def pass_block(c):
        from_mate(lambda side: row_copy(side, c, 1).wait_recv())
        passing(lambda side: pass_copy(side, c).start())

    send_block(0)
    for d in range(1, groups):
        edge_copy(d).start()
    pass_block(0)

    for d in range(1, groups):
        edge_copy(d).wait_recv()
    steps = min(HALO, groups - 1)
    right = [(groups - 1 - q, lengths[lax.rem(g + 1 + q, groups)]) for q in range(steps)]
    left = [(1 + q, lengths[lax.rem(g + groups - 1 - q, groups)]) for q in range(steps)]
    for j in range(HALO):
        source, slot, passed = right[0][0], jnp.int32(j), jnp.int32(0)
        for q in range(1, steps):
            passed = passed + right[q - 1][1]
            source = jnp.where(passed <= j, right[q][0], source)
            slot = jnp.where(passed <= j, j - passed, slot)
        halo[:, HALO + j:HALO + j + 1, :] = peers[source, :, pl.ds(slot, 1), :]
        back = HALO - j
        source, row, passed = left[0][0], HALO + jnp.minimum(left[0][1], HALO) - back, jnp.int32(0)
        for q in range(1, steps):
            passed = passed + left[q - 1][1]
            reach = passed < back
            source = jnp.where(reach, left[q][0], source)
            row = jnp.where(reach, HALO + jnp.minimum(left[q][1], HALO) - (back - passed), row)
        halo[:, j:j + 1, :] = peers[source, :, pl.ds(jnp.maximum(row, 0), 1), :]

    crossing(lambda side: halo_copy(side).start())
    to_mate(lambda side: halo_copy(side).start())
    for c in range(1, blocks):
        send_block(c)
    for copy in smalls[1:]:
        copy.wait()
    use_above = offsets[t] == t
    terms[...] = jnp.zeros_like(terms)
    for s in range(2):
        for k in range(count_k):
            terms[s, k:k + 1, 0:taps] = basis[k, t, s:s + 1, :]
    weight = jnp.concatenate([depth_weight[...], jnp.zeros((terms.shape[1] - count_k, channels), jnp.float32)], 0)
    both = [
        lax.dot_general(
            terms[s], weight, (((0,), (0,)), ((), ())),
            precision=lax.Precision.HIGHEST, preferred_element_type=jnp.float32,
        )
        for s in range(2)
    ]
    own_coef = jnp.where(use_above, both[0], both[1])
    nb_coef = jnp.where(use_above, both[1], both[0])
    for k in range(tiles):
        coef[0, k] = own_coef[:, k * LANES:(k + 1) * LANES]
        coef[1, k] = nb_coef[:, k * LANES:(k + 1) * LANES]

    def conv(source, which, k, start, n):
        total = None
        for shift in range(HALO):
            reach = n + HALO * ((taps - 1 - shift) // HALO)
            moved = source[k, start + shift:start + shift + reach, :]
            for tap in range(shift, taps, HALO):
                term = moved[tap - shift:tap - shift + n] * coef[which, k, tap:tap + 1, :]
                total = term if total is None else total + term
        return total

    def extend(target, values, c):
        first, last = span(c)

        def tile(k, carry):
            inside = first + lax.broadcasted_iota(jnp.int32, (last - first, LANES), 0) < length
            target[k, HALO + first:HALO + last, :] = jnp.where(inside, values(k, first, last), 0.0)
            return carry

        lax.fori_loop(0, tiles, tile, 0)

    def own_block(c):
        start, n = bounds[c], bounds[c + 1] - bounds[c]

        def own_tile(k, carry):
            acc[k, start:start + n, :] = raw[k, start:start + n, :] + conv(ext, 0, k, start, n)
            return carry

        lax.fori_loop(0, tiles, own_tile, 0)

    for c in range(blocks):
        extend(ext, lambda k, a, b: raw[k, a:b, :], c)

    for c in range(blocks):
        if c + 1 < blocks:
            pass_block(c + 1)
        own_block(c)

    crossed(lambda side: halo_copy(side).wait_recv())
    from_mate(lambda side: halo_copy(side).wait_recv())
    around = jnp.zeros((2 * HALO, LANES), jnp.float32)
    for k in range(tiles):
        near = jnp.where(use_above, nb_halo[1, k], nb_halo[0, k])
        from_left, from_right = None, None
        for which, values in ((0, halo[k]), (1, near)):
            lefts = jnp.concatenate([values[0:HALO], around], axis=0)
            rights = jnp.concatenate([around, values[HALO:2 * HALO]], axis=0)
            for tap in range(taps):
                factor = coef[which, k, tap:tap + 1, :]
                if tap < HALO:
                    term = lefts[tap:tap + HALO] * factor
                    from_left = term if from_left is None else from_left + term
                if tap > HALO:
                    term = rights[tap:tap + HALO] * factor
                    from_right = term if from_right is None else from_right + term
        acc[k, 0:HALO, :] += from_left
        tail[k, cap - HALO:cap, :] = from_right
    for copy in weights:
        copy.wait()

    writes = []
    for c in range(blocks):
        from_mate(lambda side: row_copy(side, c, 0).wait_recv())
        crossed(lambda side: row_copy(side, c, 0).wait_recv())
        crossed(lambda side: row_copy(side, c, 1).wait_recv())
        extend(ext_nb, lambda k, a, b: jnp.where(use_above, nb[1, k, a:b, :], nb[0, k, a:b, :]), c)

        start, n = bounds[c], bounds[c + 1] - bounds[c]

        def nb_tile(k, squares):
            state = acc[k, start:start + n, :] + conv(ext_nb, 1, k, start, n) + tail[k, pl.ds(cap + start - length, n), :]
            st[k, 0:n, :] = state
            return squares + state * state

        squares = lax.fori_loop(0, tiles, nb_tile, jnp.zeros((n, LANES), jnp.float32))
        scale = lax.rsqrt(jnp.sum(squares, axis=1, keepdims=True) * (1.0 / channels) + 1e-05)
        state = jnp.concatenate([st[k, 0:n, :] for k in range(tiles)], axis=1)
        normed = (state * scale * gain[...]).astype(jnp.bfloat16)
        total = state + b_out[...]
        for h in range(0, hidden, hid_block):
            pre = jnp.dot(normed, w_in[:, h:h + hid_block], preferred_element_type=jnp.float32) + b_in[:, h:h + hid_block]
            active = (0.5 * pre * (1.0 + lax.erf(pre * SQRT_HALF))).astype(jnp.bfloat16)
            total = total + jnp.dot(active, w_out[h:h + hid_block, :], preferred_element_type=jnp.float32)
        inside = start + lax.broadcasted_iota(jnp.int32, total.shape, 0) < length
        out_buf[start:start + n, :] = jnp.where(inside, total, 0.0)
        write = pltpu.make_async_copy(
            out_buf.at[pl.ds(start, n), :], out_hbm.at[0, pl.ds(start, n), :], out_sem.at[c]
        )
        write.start()
        writes.append(write)

    for d in range(1, groups):
        edge_copy(d).wait_send()
    crossing(lambda side: halo_copy(side).wait_send())
    to_mate(lambda side: halo_copy(side).wait_send())
    for c in range(blocks):
        crossing(lambda side: row_copy(side, c, 0).wait_send())
        to_mate(lambda side: row_copy(side, c, 0).wait_send())
        to_mate(lambda side: row_copy(side, c, 1).wait_send())
        passing(lambda side: pass_copy(side, c).wait_send())
    for write in writes:
        write.wait()


def hand_over(rows, source, target, held, in_sem, out_sem):
    pieces = [pl.ds(first, rows) for first in range(0, held.shape[0], rows)]
    takes = [pltpu.make_async_copy(source.at[0, piece, :], held.at[piece, :], in_sem.at[i]) for i, piece in enumerate(pieces)]
    gives = [pltpu.make_async_copy(held.at[piece, :], target.at[0, piece, :], out_sem.at[i]) for i, piece in enumerate(pieces)]
    for take in takes:
        take.start()
    for take, give in zip(takes, gives):
        take.wait()
        give.start()
    for give in gives:
        give.wait()


def on_device(groups, lat_count, field, piece_lengths, offsets, basis, depth_weight, gain, w_in, b_in, w_out, b_out):
    rows_dev, slot_cap, channels = field.shape
    assert rows_dev == 1 and lat_count % 2 == 0 and basis.shape[2] == 2 and basis.shape[3] == 2 * HALO + 1
    cap = round_up(slot_cap, 8)
    if cap != slot_cap:
        field = jnp.pad(field, ((0, 0), (0, cap - slot_cap), (0, 0)))
    tiles = channels // LANES
    hidden = w_in.shape[1]
    third = cap // 3
    bounds = (0, third, 2 * third, cap) if cap % 24 == 0 else (0, cap)
    blocks = len(bounds) - 1
    n = max(bounds[c + 1] - bounds[c] for c in range(blocks))
    hid_block = 256 if hidden % 256 == 0 else LANES
    taps = basis.shape[3]
    k_rows = round_up(basis.shape[0], 8)
    hbm = pl.BlockSpec(memory_space=pltpu.HBM)
    f32 = jnp.float32
    out = pl.pallas_call(
        functools.partial(kernel, groups, lat_count, bounds, hid_block),
        out_shape=jax.ShapeDtypeStruct((1, cap, channels), f32),
        in_specs=[hbm] * 10,
        out_specs=pl.BlockSpec(memory_space=pl.ANY),
        scratch_shapes=[
            pltpu.SMEM(piece_lengths.shape, jnp.int32),
            pltpu.SMEM(offsets.shape, jnp.int32),
            pltpu.VMEM(basis.shape, f32),
            pltpu.VMEM(depth_weight.shape, f32),
            pltpu.VMEM((1, channels), f32),
            pltpu.VMEM((1, hidden), f32),
            pltpu.VMEM((1, channels), f32),
            pltpu.VMEM((tiles, cap, LANES), f32),
            pltpu.VMEM((tiles, 2 * HALO, LANES), f32),
            pltpu.VMEM((groups, tiles, 2 * HALO, LANES), f32),
            pltpu.VMEM((tiles, 2 * HALO, LANES), f32),
            pltpu.VMEM((2, tiles, cap, LANES), f32),
            pltpu.VMEM((2, tiles, 2 * HALO, LANES), f32),
            pltpu.VMEM((tiles, cap + 2 * HALO, LANES), f32),
            pltpu.VMEM((tiles, cap + 2 * HALO, LANES), f32),
            pltpu.VMEM((tiles, 2 * cap + 2 * HALO, LANES), f32),
            pltpu.VMEM((2, k_rows, round_up(taps, 8)), f32),
            pltpu.VMEM((2, tiles, round_up(taps, 8), LANES), f32),
            pltpu.VMEM((tiles, cap, LANES), f32),
            pltpu.VMEM((tiles, n, LANES), f32),
            pltpu.VMEM((cap, channels), f32),
            pltpu.VMEM(w_in.shape, w_in.dtype),
            pltpu.VMEM(w_out.shape, w_out.dtype),
            pltpu.SemaphoreType.DMA((tiles,)),
            pltpu.SemaphoreType.DMA((7,)),
            pltpu.SemaphoreType.DMA((2,)),
            pltpu.SemaphoreType.DMA((groups,)),
            pltpu.SemaphoreType.DMA((groups,)),
            pltpu.SemaphoreType.DMA((2,)),
            pltpu.SemaphoreType.DMA((2,)),
            pltpu.SemaphoreType.DMA((2, blocks, 2)),
            pltpu.SemaphoreType.DMA((2, blocks, 2)),
            pltpu.SemaphoreType.DMA((blocks,)),
            pltpu.SemaphoreType.DMA((blocks,)),
        ],
        compiler_params=pltpu.CompilerParams(
            collective_id=0, has_side_effects=True, vmem_limit_bytes=63 * 1024 * 1024
        ),
        cost_estimate=pl.CostEstimate(flops=4 * cap * channels * hidden, bytes_accessed=6 * 1024 * 1024, transcendentals=0),
    )(
        piece_lengths, offsets, field, basis, depth_weight, gain, w_in, b_in, w_out, b_out,
    )
    rows = block_rows(cap, 72)
    out = pl.pallas_call(
        functools.partial(hand_over, rows),
        out_shape=jax.ShapeDtypeStruct(out.shape, f32),
        in_specs=[hbm],
        out_specs=hbm,
        scratch_shapes=[
            pltpu.VMEM((cap, channels), f32),
            pltpu.SemaphoreType.DMA((cap // rows,)),
            pltpu.SemaphoreType.DMA((cap // rows,)),
        ],
        compiler_params=pltpu.CompilerParams(vmem_limit_bytes=63 * 1024 * 1024),
    )(out)
    return out[:, :slot_cap, :]


def solution(mesh):
    placed = (P(("ens", "lat"), "lon", None), P(), P(), P(), P(), P(), P(), P(), P(), P())
    return jax.shard_map(
        functools.partial(on_device, mesh.shape["lon"], mesh.shape["lat"]),
        mesh=mesh,
        in_specs=placed,
        out_specs=P(("ens", "lat"), "lon", None),
        check_vma=False,
    )
```
